128 devices in a mesh: row: 8 (over y, core), col: 16 (over z, x).
Axes of the slice: x: 4, y: 4, z: 4, core: 2. Of those that a mesh axis runs over, the one named last changes fastest.
Arguments:
- amplitudes: bfloat16 [6144, 2048], P(('row', 'col')), may hold values from -6 to 6
- integrals: bfloat16 [128, 16, 8, 128, 128], P(('row', 'col')), may hold values from -0.25 to 0.25
- slot_index: int32 [128, 16, 8, 2], P(('row', 'col')), may hold values from 0 to 47, as said below
- virt_energy: float32 [3072], P(('row', 'col')), may hold values from 0.3 to 3
- b_energy: float32 [2], replicated, may hold values from 0.3 to 3
- pair_energy: float32 [2048], replicated, may hold values from -3 to -0.5
Outputs:
- update: float32 [2, 3072, 2048], P(None, ('row', 'col'))
The draws below stay inside these ranges and needn't reach their ends.
Inputs may be any that keep to these rules, and one draw needn't show every extreme that they name: `slot_index`: A device sends at most 8 filled slots to each member of its row group, filled slots first; in every row group one member receives 8 filled slots from every device of the group, and one device holds 8 filled slots for every member; filled and empty slots both occur.
All inputs are finite; a program needn't handle non-finite values.
Results may differ from the reference program's by a relative error of at most 0.0003.
Values may be sent and summed in bfloat16 or wider, within the bound.
A program may use at most 128 MiB of HBM per device.

```python
import jax
import jax.numpy as jnp
from jax import lax

TILE = 128
NT = 24
PAIRS = 2048
NB = 2
ND = 2
CAP = 8
VIRT = 3072
N_ROW = 8
N_COL = 16
DEVICES = 128


def draw_slot_index(key, part):
    key = jax.random.fold_in(key, 11)
    keys = jax.random.split(key, 6)
    a_local = NT // N_ROW
    shift = jax.random.randint(keys[0], (N_ROW, N_COL), 1, 4)
    heavy = jax.random.randint(keys[5], (N_ROW, 1), 0, N_COL)
    is_heavy = heavy == jnp.arange(N_COL)[None, :]
    weight = jnp.where(is_heavy, 16, 16 // 2 ** shift).reshape(DEVICES, 1)
    jitter = jax.random.randint(keys[1], (DEVICES, N_COL), 0, 2)
    count = jnp.clip(weight * CAP // 16 - jitter, 0, CAP)
    count = jnp.where(weight == 16, CAP, count)
    target = jax.random.randint(keys[2], (N_ROW, 1), 0, N_COL)
    full = jnp.repeat(target, N_COL, axis=0) == jnp.arange(N_COL)[None, :]
    count = jnp.where(full, CAP, count)
    live = jnp.arange(CAP)[None, None, :] < count[:, :, None]
    out_slot = jax.random.randint(keys[3], (DEVICES, N_COL, CAP), 0, NB * a_local)
    out_slot = jnp.where(live, out_slot, NB * a_local)
    amp_tile = jax.random.randint(keys[4], (DEVICES, N_COL, CAP), 0, ND * NT)
    return jnp.stack([out_slot, amp_tile], axis=-1).astype(jnp.int32)


def block_scale(own_key, shape, pieces, least, largest):
    gain, own = 1.0, jax.random.fold_in(own_key, 6)
    for dim, blocks in pieces:
        heights = jnp.exp(jax.random.uniform(jax.random.fold_in(own, dim), (blocks,), jnp.float32, least / len(pieces), largest / len(pieces)))
        gain = gain * jnp.repeat(heights, shape[dim] // blocks).reshape([-1 if axis == dim else 1 for axis in range(len(shape))])
    return gain


def centred(stream_key, extent, spread, reach, pieces=(), kind=jnp.bfloat16):
    result = jax.random.normal(stream_key, extent, jnp.float32) * spread
    if len(pieces) > 0:
        result = block_scale(stream_key, extent, pieces, -0.22, 0.18) * result
    return jnp.clip(result, min=-reach, max=reach).astype(kind)


def setup_inputs(seed: int = 0) -> dict:
    arg_keys = jax.random.split(jax.random.key(seed), 7)
    amplitudes = centred(arg_keys[0], (ND * NT * TILE, PAIRS), 1.0, 6.0, ((0, 128),))
    integrals = centred(arg_keys[1], (DEVICES, N_COL, CAP, TILE, TILE), (N_COL * CAP * TILE // (6 * NB * (NT // N_ROW))) ** -0.5, 0.25, ((0, 128),))
    slot_index = draw_slot_index(jax.random.fold_in(arg_keys[6], 71), 0)
    virt_energy = jnp.clip(0.3 + 2.7 * jax.random.uniform(arg_keys[3], (VIRT,), jnp.float32) ** block_scale(arg_keys[3], (VIRT,), ((0, 128),), -0.2, 0.2), 0.3, 3.0)
    b_energy = jnp.clip(jax.random.uniform(arg_keys[4], (NB,), jnp.float32, 0.3, 3.0), 0.3, 3.0)
    pair_energy = jnp.clip(jax.random.uniform(arg_keys[5], (PAIRS,), jnp.float32, -3.0, -0.5), -3.0, -0.5)
    return dict(amplitudes=amplitudes, integrals=integrals, slot_index=slot_index, virt_energy=virt_energy, b_energy=b_energy, pair_energy=pair_energy)


def reference(amplitudes, integrals, slot_index, virt_energy, b_energy, pair_energy):
    a_local = NT // N_ROW
    amp_tiles = amplitudes.astype(jnp.float32).reshape(ND * NT, TILE, PAIRS)
    devices_ids = jnp.arange(DEVICES, dtype=jnp.int32)

    def per_device(total, item):
        tiles, index, device = item
        group = device // N_COL

        def per_member(acc, inner):
            member_tiles, member_index = inner
            out_slot = member_index[:, 0]
            operand = jnp.take(amp_tiles, member_index[:, 1], axis=0)
            contrib = jnp.einsum("sac,scp->sap", member_tiles.astype(jnp.float32), operand,
                                 precision=lax.Precision.HIGHEST)
            target = (out_slot // a_local) * NT + group * a_local + out_slot % a_local
            target = jnp.where(out_slot == NB * a_local, NB * NT, target).astype(jnp.int32)
            return acc.at[target].add(contrib), None

        total, unused = lax.scan(per_member, total, (tiles, index))
        return total, None

    start = jnp.zeros((NB * NT + 1, TILE, PAIRS), jnp.float32)
    total, unused = lax.scan(per_device, start, (integrals, slot_index, devices_ids))
    ladder = total[:NB * NT].reshape(NB, NT * TILE, PAIRS)
    denom = virt_energy[None, :, None] + b_energy[:, None, None] - pair_energy[None, None, :]
    return ladder / denom
```

```python
import jax
import jax.numpy as jnp
from jax import lax
from jax.experimental import pallas as pl
from jax.experimental.pallas import tpu as pltpu
from jax.sharding import PartitionSpec as P

NT = 24
NB = 2
TILE = 128
GROUP = 4
WIDTH = 512


def slot_kernel(n_out, n_slot, out_idx, amp_idx, tiles, amps, partial, order, amp_of, first, fill):
    @pl.when(pl.program_id(0) == 0)
    def _():
        for o in range(n_out + 1):
            fill[o] = 0

        def count(s, carry):
            o = out_idx[s]
            fill[o] = fill[o] + 1
            return carry

        lax.fori_loop(0, n_slot, count, 0)
        start = jnp.int32(0)
        for o in range(n_out):
            first[o] = start
            start = start + lax.div(fill[o] + (GROUP - 1), GROUP)
            fill[o] = first[o] * GROUP
        first[n_out] = start
        fill[n_out] = start * GROUP

        def blank(p, carry):
            order[p] = n_slot
            amp_of[p] = 0
            return carry

        lax.fori_loop(0, start * GROUP, blank, 0)

        def place(s, carry):
            o = out_idx[s]

            @pl.when(o < n_out)
            def _():
                p = fill[o]
                order[p] = s
                amp_of[p] = amp_idx[s]
                fill[o] = p + 1

            return carry

        lax.fori_loop(0, n_slot, place, 0)

    for o in range(n_out):
        partial[o] = jnp.zeros(partial.shape[1:], jnp.float32)

        def step(q, carry):
            left = []
            for g in range(GROUP):
                s = order[q * GROUP + g]
                tile = tiles[lax.min(s, n_slot - 1)]
                left.append(jnp.where(s < n_slot, tile, jnp.zeros_like(tile)))
            right = [amps[amp_of[q * GROUP + g]] for g in range(GROUP)]
            partial[o] += jnp.dot(
                jnp.concatenate(left, axis=1), jnp.concatenate(right, axis=0), preferred_element_type=jnp.float32
            )
            return carry

        lax.fori_loop(first[o], first[o + 1], step, 0)


def slot_products(tiles, out_idx, amp_idx, amps):
    n_slot = tiles.shape[0]
    n_out = NB * 3
    pairs = amps.shape[2]
    room = n_slot + n_out * GROUP

    def kern(oi, ai, t, a, p, *scratch):
        slot_kernel(n_out, n_slot, oi, ai, t, a, p, *scratch)

    return pl.pallas_call(
        kern,
        grid=(pairs // WIDTH,),
        out_shape=jax.ShapeDtypeStruct((n_out, TILE, pairs), jnp.float32),
        in_specs=[
            pl.BlockSpec(memory_space=pltpu.SMEM),
            pl.BlockSpec(memory_space=pltpu.SMEM),
            pl.BlockSpec(memory_space=pltpu.VMEM),
            pl.BlockSpec((amps.shape[0], TILE, WIDTH), lambda i: (0, 0, i)),
        ],
        out_specs=pl.BlockSpec((n_out, TILE, WIDTH), lambda i: (0, 0, i)),
        scratch_shapes=[
            pltpu.SMEM((room,), jnp.int32),
            pltpu.SMEM((room,), jnp.int32),
            pltpu.SMEM((n_out + 1,), jnp.int32),
            pltpu.SMEM((n_out + 1,), jnp.int32),
        ],
        compiler_params=pltpu.CompilerParams(vmem_limit_bytes=56 * 1024 * 1024),
        name="slot_products",
    )(out_idx, amp_idx, tiles, amps)


def per_device(amplitudes, integrals, slot_index, virt_energy, b_energy, pair_energy):
    whole = lax.all_gather(amplitudes, ("row", "col"), axis=0, tiled=True)
    pairs = whole.shape[1]
    amp_tiles = whole.reshape(-1, TILE, pairs)
    a_local = NT // lax.axis_size("row")
    index = slot_index.reshape(-1, 2)
    tiles = integrals.reshape(-1, TILE, TILE)
    partial = slot_products(tiles, index[:, 0], index[:, 1], amp_tiles)
    ladder_rows = partial.reshape(NB, a_local * TILE, pairs)
    owned = lax.psum_scatter(ladder_rows, "col", scatter_dimension=1, tiled=True)
    denom = virt_energy[None, :, None] + b_energy[:, None, None] - pair_energy[None, None, :]
    return owned / denom


def solution(mesh):
    placed = (
        P(("row", "col"), None),
        P(("row", "col"), None, None, None, None),
        P(("row", "col"), None, None, None),
        P(("row", "col")),
        P(),
        P(),
    )
    return jax.shard_map(
        per_device,
        mesh=mesh,
        in_specs=placed,
        out_specs=P(None, ("row", "col"), None),
        check_vma=False,
    )
```

```python
import functools

import jax
import jax.numpy as jnp
from jax import lax
from jax.experimental import pallas as pl
from jax.experimental.pallas import tpu as pltpu
from jax.sharding import PartitionSpec as P

MESH = pl.DeviceIdType.MESH
NT = 24
NB = 2
TILE = 128
SLOTS = 128
OUTS = 6
GROUP = 4
QUADS = 36
LANES = 128
SUBS = 8
CHUNKS = 4
WIDE = LANES * SUBS // CHUNKS
OWN = 24
ROWS = 48
RING = 4
Y, Z, X = 0, 1, 2
ORDERS = (
    (X, Z, Y), (Y, Z, X),
    (Z, X, Y), (Y, X, Z),
    (X, Z, Y), (Y, Z, X),
    (Z, X, Y), (Y, X, Z),
)
SUM_ORDERS = ((X, Z), (Z, X), (X, Z), (Z, X))


def list_kernel(out_idx, amp_idx, lists, fill, first):
    for o in range(OUTS + 1):
        fill[o] = 0

    def count(s, carry):
        o = out_idx[s]
        fill[o] = fill[o] + 1
        return carry

    lax.fori_loop(0, SLOTS, count, 0, unroll=4)

    def blank(q, carry):
        for g in range(GROUP):
            lists[g, q] = SLOTS
            lists[GROUP + g, q] = 0
        lists[0, 64 + q] = q
        return carry

    lax.fori_loop(0, QUADS, blank, 0, unroll=2)
    start = jnp.int32(0)
    for o in range(OUTS):
        here = lax.div(fill[o] + (GROUP - 1), GROUP)
        first[o] = start * GROUP

        @pl.when(here > 0)
        def _():
            lists[0, 64 + start] = 0

        start = start + here
        lists[1, 64 + o] = jnp.where(here > 0, start, 0)

    def place(s, carry):
        o = out_idx[s]

        @pl.when(o < OUTS)
        def _():
            p = first[o]
            q = lax.div(p, GROUP)
            g = p - q * GROUP
            lists[g, q] = s
            lists[GROUP + g, q] = amp_idx[s]
            first[o] = p + 1

        return carry

    lax.fori_loop(0, SLOTS, place, 0, unroll=2)


def slot_lists(out_idx, amp_idx):
    return pl.pallas_call(
        list_kernel,
        out_shape=jax.ShapeDtypeStruct((8, 128), jnp.int32),
        in_specs=[pl.BlockSpec(memory_space=pltpu.SMEM)] * 2,
        out_specs=pl.BlockSpec(memory_space=pltpu.SMEM),
        scratch_shapes=[pltpu.SMEM((8,), jnp.int32), pltpu.SMEM((8,), jnp.int32)],
        name="slot_lists",
    )(out_idx, amp_idx)


def ladder_kernel(lists, lists_hbm, amps, tiles, owned, *scratch):
    slices = scratch[:SUBS]
    gathered = [ref.reshape(4, 2, 4, 4, ROWS, LANES) for ref in slices]
    (tiles_own, tiles_sib, history, part, got1, sum1, got2, cross_out, cross_in, lists_in, lists_sib,
     send0, recv0, local0, send_ag, recv_ag, send1, recv1, send2, recv2, send_x, recv_x, misc) = scratch[SUBS:]
    row, col = lax.axis_index("row"), lax.axis_index("col")
    y, core = lax.div(row, 2), lax.rem(row, 2)
    z, x = lax.div(col, RING), lax.rem(col, RING)
    at = (y, z, x)
    sib = (y * 2 + 1 - core, col)

    def turn(value, by):
        return lax.rem(value + by + RING, RING)

    def peer(axis, by):
        place = list(at)
        place[axis] = turn(at[axis], by)
        return (place[Y] * 2 + core, place[Z] * RING + place[X])

    partners = [peer(a, d) for a in (Y, Z, X) for d in (1, -1)] + [peer(Z, 2), peer(X, 2), sib]
    barrier = pltpu.get_barrier_semaphore()
    for partner in partners:
        pl.semaphore_signal(barrier, inc=1, device_id=partner, device_id_type=MESH)
    pl.semaphore_wait(barrier, len(partners))

    sent = []

    def send(src, dst, s_sem, r_sem, to):
        copy = pltpu.make_async_remote_copy(
            src_ref=src, dst_ref=dst, send_sem=s_sem, recv_sem=r_sem, device_id=to, device_id_type=MESH
        )
        copy.start()
        sent.append(copy)

    def arrive(dst, s_sem, r_sem, to):
        pltpu.make_async_remote_copy(
            src_ref=dst, dst_ref=dst, send_sem=s_sem, recv_sem=r_sem, device_id=to, device_id_type=MESH
        ).wait_recv()

    here = []
    for s in range(SUBS):
        mine = pl.ds(pl.multiple_of(core * (SUBS * LANES) + s * LANES, LANES), LANES)
        other = pl.ds(pl.multiple_of((1 - core) * (SUBS * LANES) + s * LANES, LANES), LANES)
        home = gathered[s].at[y, core, z, x]
        send(amps.at[:, other], home, send0.at[s], recv0.at[s], sib)
        copy = pltpu.make_async_copy(amps.at[:, mine], home, local0.at[s])
        copy.start()
        here.append(copy)
    send(lists_hbm, lists_in, misc.at[0], misc.at[1], sib)
    send(tiles, tiles_sib.at[pl.ds(0, SLOTS)], misc.at[2], misc.at[3], sib)
    own_tiles = pltpu.make_async_copy(tiles, tiles_own.at[pl.ds(0, SLOTS)], misc.at[4])
    own_tiles.start()
    for ref in (tiles_own, tiles_sib):
        ref[SLOTS] = jnp.zeros((TILE, TILE), ref.dtype)
    history[0] = jnp.zeros((TILE, WIDE), jnp.float32)

    def region(s, phase, index, half):
        axis = ORDERS[s][phase]
        done = ORDERS[s][:phase]
        pick = [slice(None) if a in done else at[a] for a in (Y, Z, X)]
        pick[axis] = index
        return gathered[s].at[pick[Y], half, pick[Z], pick[X]]

    def spread(s, phase):
        axis = ORDERS[s][phase]
        mine = region(s, phase, at[axis], slice(None))
        for way, by in enumerate((1, -1)):
            n = phase * 4 + way
            send(mine, mine, send_ag.at[s, n], recv_ag.at[s, n], peer(axis, by))

    def forward(s, phase):
        axis = ORDERS[s][phase]
        for way, by in enumerate((1, -1)):
            n = phase * 4 + way
            index = turn(at[axis], -by)
            arrive(region(s, phase, index, slice(None)), send_ag.at[s, n], recv_ag.at[s, n], peer(axis, by))
            passed = region(s, phase, index, way)
            send(passed, passed, send_ag.at[s, n + 2], recv_ag.at[s, n + 2], peer(axis, by))

    def finish(s, phase):
        axis = ORDERS[s][phase]
        for way, by in enumerate((1, -1)):
            n = phase * 4 + 2 + way
            arrive(region(s, phase, turn(at[axis], 2), way), send_ag.at[s, n], recv_ag.at[s, n], peer(axis, by))

    for s in range(SUBS):
        here[s].wait()
        arrive(gathered[s].at[y, 1 - core, z, x], send0.at[s], recv0.at[s], sib)
        spread(s, 0)
    for phase in (0, 1):
        for s in range(SUBS):
            forward(s, phase)
        for s in range(SUBS):
            finish(s, phase)
            spread(s, phase + 1)

    own_tiles.wait()
    arrive(tiles_sib.at[pl.ds(0, SLOTS)], misc.at[2], misc.at[3], sib)
    arrive(lists_in, misc.at[0], misc.at[1], sib)
    to_scalar = pltpu.make_async_copy(lists_in, lists_sib, misc.at[5])
    to_scalar.start()
    to_scalar.wait()

    def products(k, group):
        which, tile_ref = ((lists, tiles_own), (lists_sib, tiles_sib))[group]
        per = SUBS // CHUNKS
        parts = slices[k * per : (k + 1) * per]

        def step(q, carry):
            left, right = [], []
            for g in range(GROUP):
                left.append(tile_ref[which[g, q]])
                m = which[GROUP + g, q]
                right.append(jnp.concatenate([ref[m] for ref in parts], axis=1))
            new = jnp.dot(
                jnp.concatenate(left, axis=1), jnp.concatenate(right, axis=0), preferred_element_type=jnp.float32
            )
            history[q + 1] = history[which[0, 64 + q]] + new
            return carry

        lax.fori_loop(0, QUADS, step, 0, unroll=2)
        rows_ref = part.at[k, group].reshape(OUTS * TILE, WIDE)
        for o in range(OUTS):
            rows_ref[o * TILE : (o + 1) * TILE, :] = history[which[1, 64 + o]]

    def pick_axis(ref, axis, index):
        return ref.at[:, :, index] if axis == Z else ref.at[:, :, :, index]

    steps = (1, -1, 2)

    def sum_send1(k):
        axis = SUM_ORDERS[k][0]
        for n, by in enumerate(steps):
            src = pick_axis(part.at[k], axis, turn(at[axis], by))
            send(src, got1.at[k, n], send1.at[k, n], recv1.at[k, n], peer(axis, by))

    def sum_step2(k):
        axis, then = SUM_ORDERS[k]
        for n, by in enumerate(steps):
            arrive(got1.at[k, n], send1.at[k, n], recv1.at[k, n], peer(axis, by))
        for g in range(2):
            for b in range(NB):
                for i in range(RING):
                    own = part[k, g, b, at[Z], i] if axis == Z else part[k, g, b, i, at[X]]
                    sum1[k, g, b, i] = (own + got1[k, 0, g, b, i]) + (got1[k, 1, g, b, i] + got1[k, 2, g, b, i])
        for n, by in enumerate(steps):
            src = sum1.at[k, :, :, turn(at[then], by)]
            send(src, got2.at[k, n], send2.at[k, n], recv2.at[k, n], peer(then, by))

    def sum_step3(k):
        then = SUM_ORDERS[k][1]
        for n, by in enumerate(steps):
            arrive(got2.at[k, n], send2.at[k, n], recv2.at[k, n], peer(then, by))
        for g in (1, 0):
            for b in range(NB):
                total = (sum1[k, g, b, at[then]] + got2[k, 0, g, b]) + (got2[k, 1, g, b] + got2[k, 2, g, b])
                if g == 1:
                    cross_out[k, b] = total
                else:
                    columns = pl.ds(pl.multiple_of(core * (SUBS * LANES) + k * WIDE, WIDE), WIDE)
                    owned[b, :, columns] = total
            if g == 1:
                send(cross_out.at[k], cross_in.at[k], send_x.at[k], recv_x.at[k], sib)

    def sum_step4(k):
        arrive(cross_in.at[k], send_x.at[k], recv_x.at[k], sib)
        for b in range(NB):
            columns = pl.ds(pl.multiple_of((1 - core) * (SUBS * LANES) + k * WIDE, WIDE), WIDE)
            owned[b, :, columns] = cross_in[k, b]

    per = SUBS // CHUNKS
    for s in range(per):
        forward(s, 2)
    for k in range(CHUNKS):
        for s in range(k * per, (k + 1) * per):
            finish(s, 2)
        products(k, 0)
        if k + 1 < CHUNKS:
            for s in range((k + 1) * per, (k + 2) * per):
                forward(s, 2)
        if k >= 1:
            sum_step2(k - 1)
        products(k, 1)
        sum_send1(k)
        if k >= 1:
            sum_step3(k - 1)
    sum_step2(CHUNKS - 1)
    sum_step3(CHUNKS - 1)
    for k in range(CHUNKS):
        sum_step4(k)
    for copy in sent:
        copy.wait_send()


def owned_ladder(lists, amplitudes, tiles):
    dma = pltpu.SemaphoreType.DMA
    vmem = pltpu.VMEM
    f32 = jnp.float32
    scratch = [vmem((2 * NT, TILE, LANES), jnp.bfloat16) for _ in range(SUBS)]
    scratch += [
        vmem((SLOTS + 1, TILE, TILE), jnp.bfloat16),
        vmem((SLOTS + 1, TILE, TILE), jnp.bfloat16),
        vmem((QUADS + 1, TILE, WIDE), f32),
        vmem((CHUNKS, 2, NB, RING, RING, OWN, WIDE), f32),
        vmem((CHUNKS, 3, 2, NB, RING, OWN, WIDE), f32),
        vmem((CHUNKS, 2, NB, RING, OWN, WIDE), f32),
        vmem((CHUNKS, 3, 2, NB, OWN, WIDE), f32),
        vmem((CHUNKS, NB, OWN, WIDE), f32),
        vmem((CHUNKS, NB, OWN, WIDE), f32),
        vmem((8, 128), jnp.int32),
        pltpu.SMEM((8, 128), jnp.int32),
        dma((SUBS,)), dma((SUBS,)), dma((SUBS,)),
        dma((SUBS, 12)), dma((SUBS, 12)),
        dma((CHUNKS, 3)), dma((CHUNKS, 3)), dma((CHUNKS, 3)), dma((CHUNKS, 3)),
        dma((CHUNKS,)), dma((CHUNKS,)), dma((6,)),
    ]
    return pl.pallas_call(
        ladder_kernel,
        out_shape=jax.ShapeDtypeStruct((NB, OWN, 2 * SUBS * LANES), f32),
        in_specs=[
            pl.BlockSpec(memory_space=pltpu.SMEM),
            pl.BlockSpec(memory_space=pl.ANY),
            pl.BlockSpec(memory_space=pl.ANY),
            pl.BlockSpec(memory_space=pl.ANY),
        ],
        out_specs=pl.BlockSpec(memory_space=pltpu.VMEM),
        scratch_shapes=scratch,
        compiler_params=pltpu.CompilerParams(
            collective_id=0, has_side_effects=True, vmem_limit_bytes=60 * 1024 * 1024
        ),
        name="ladder",
    )(lists, lists, amplitudes, tiles)


def per_device(amplitudes, integrals, slot_index, virt_energy, b_energy, pair_energy):
    index = slot_index.reshape(-1, 2)
    tiles = integrals.reshape(-1, TILE, TILE)
    lists = slot_lists(index[:, 0], index[:, 1])
    owned = owned_ladder(lists, amplitudes, tiles)
    denom = virt_energy[None, :, None] + b_energy[:, None, None] - pair_energy[None, None, :]
    return owned / denom


def solution(mesh):
    placed = (
        P(("row", "col"), None),
        P(("row", "col"), None, None, None, None),
        P(("row", "col"), None, None, None),
        P(("row", "col")),
        P(),
        P(),
    )
    return jax.shard_map(
        per_device,
        mesh=mesh,
        in_specs=placed,
        out_specs=P(None, ("row", "col"), None),
        check_vma=False,
    )
```

```python
import functools

import jax
import jax.numpy as jnp
from jax import lax
from jax.experimental import pallas as pl
from jax.experimental.pallas import tpu as pltpu
from jax.sharding import PartitionSpec as P

MESH = pl.DeviceIdType.MESH
NT = 24
NB = 2
TILE = 128
SLOTS = 128
OUTS = 6
GROUP = 4
QUADS = 36
LANES = 128
SUBS = 8
CHUNKS = 4
WIDE = LANES * SUBS // CHUNKS
OWN = 24
ROWS = 48
RING = 4
Y, Z, X = 0, 1, 2
ORDERS = (
    (X, Z, Y), (Z, Y, X),
    (Z, X, Y), (X, Y, Z),
    (Z, Y, X), (X, Y, Z),
    (X, Z, Y), (Z, X, Y),
)
SUM_ORDERS = ((X, Z), (Z, X))


def list_kernel(out_idx, amp_idx, lists, fill, first):
    for o in range(OUTS + 1):
        fill[o] = 0

    def count(s, carry):
        o = out_idx[s]
        fill[o] = fill[o] + 1
        return carry

    lax.fori_loop(0, SLOTS, count, 0, unroll=4)

    def blank(q, carry):
        for g in range(GROUP):
            lists[g, q] = SLOTS
            lists[GROUP + g, q] = 0
        lists[0, 64 + q] = q
        return carry

    lax.fori_loop(0, QUADS, blank, 0, unroll=2)
    start = jnp.int32(0)
    for o in range(OUTS):
        here = lax.div(fill[o] + (GROUP - 1), GROUP)
        first[o] = start * GROUP

        @pl.when(here > 0)
        def _():
            lists[0, 64 + start] = 0

        start = start + here
        lists[1, 64 + o] = jnp.where(here > 0, start, 0)

    def place(s, carry):
        o = out_idx[s]

        @pl.when(o < OUTS)
        def _():
            p = first[o]
            q = lax.div(p, GROUP)
            g = p - q * GROUP
            lists[g, q] = s
            lists[GROUP + g, q] = amp_idx[s]
            first[o] = p + 1

        return carry

    lax.fori_loop(0, SLOTS, place, 0, unroll=2)


def slot_lists(out_idx, amp_idx):
    return pl.pallas_call(
        list_kernel,
        out_shape=jax.ShapeDtypeStruct((8, 128), jnp.int32),
        in_specs=[pl.BlockSpec(memory_space=pltpu.SMEM)] * 2,
        out_specs=pl.BlockSpec(memory_space=pltpu.SMEM),
        scratch_shapes=[pltpu.SMEM((8,), jnp.int32), pltpu.SMEM((8,), jnp.int32)],
        name="slot_lists",
    )(out_idx, amp_idx)


def ladder_kernel(lists, lists_hbm, amps, tiles, owned, *scratch):
    slices = scratch[:SUBS]
    gathered = [ref.reshape(4, 2, 4, 4, ROWS, LANES) for ref in slices]
    (tiles_own, tiles_sib, history, part, relay, got1, sum1, got2, cross_out, cross_in, lists_in, lists_sib,
     send0, recv0, local0, send_ag, recv_ag, send1, recv1, send2, recv2, send_x, recv_x, misc) = scratch[SUBS:]
    row, col = lax.axis_index("row"), lax.axis_index("col")
    y, core = lax.div(row, 2), lax.rem(row, 2)
    z, x = lax.div(col, RING), lax.rem(col, RING)
    at = (y, z, x)
    sib = (y * 2 + 1 - core, col)

    def turn(value, by):
        return lax.rem(value + by + RING, RING)

    def peer(axis, by):
        place = list(at)
        place[axis] = turn(at[axis], by)
        return (place[Y] * 2 + core, place[Z] * RING + place[X])

    partners = [peer(a, d) for a in (Y, Z, X) for d in (1, -1)] + [peer(a, 2) for a in (Y, Z, X)] + [sib]
    barrier = pltpu.get_barrier_semaphore()
    for partner in partners:
        pl.semaphore_signal(barrier, inc=1, device_id=partner, device_id_type=MESH)
    pl.semaphore_wait(barrier, len(partners))

    sent = []

    def send(src, dst, s_sem, r_sem, to):
        copy = pltpu.make_async_remote_copy(
            src_ref=src, dst_ref=dst, send_sem=s_sem, recv_sem=r_sem, device_id=to, device_id_type=MESH
        )
        copy.start()
        sent.append(copy)

    def arrive(dst, s_sem, r_sem, to):
        pltpu.make_async_remote_copy(
            src_ref=dst, dst_ref=dst, send_sem=s_sem, recv_sem=r_sem, device_id=to, device_id_type=MESH
        ).wait_recv()

    here = []
    for s in range(SUBS):
        mine = pl.ds(pl.multiple_of(core * (SUBS * LANES) + s * LANES, LANES), LANES)
        other = pl.ds(pl.multiple_of((1 - core) * (SUBS * LANES) + s * LANES, LANES), LANES)
        home = gathered[s].at[y, core, z, x]
        send(amps.at[:, other], home, send0.at[s], recv0.at[s], sib)
        copy = pltpu.make_async_copy(amps.at[:, mine], home, local0.at[s])
        copy.start()
        here.append(copy)
    send(lists_hbm, lists_in, misc.at[0], misc.at[1], sib)
    send(tiles, tiles_sib.at[pl.ds(0, SLOTS)], misc.at[2], misc.at[3], sib)
    own_tiles = pltpu.make_async_copy(tiles, tiles_own.at[pl.ds(0, SLOTS)], misc.at[4])
    own_tiles.start()
    for ref in (tiles_own, tiles_sib):
        ref[SLOTS] = jnp.zeros((TILE, TILE), ref.dtype)
    history[0] = jnp.zeros((TILE, WIDE), jnp.float32)

    def region(s, phase, index, half):
        axis = ORDERS[s][phase]
        done = ORDERS[s][:phase]
        pick = [slice(None) if a in done else at[a] for a in (Y, Z, X)]
        pick[axis] = index
        return gathered[s].at[pick[Y], half, pick[Z], pick[X]]

    steps = (1, -1, 2)

    def spread(s, phase):
        axis = ORDERS[s][phase]
        mine = region(s, phase, at[axis], slice(None))
        for n, by in enumerate(steps):
            send(mine, mine, send_ag.at[s, phase * 3 + n], recv_ag.at[s, phase * 3 + n], peer(axis, by))

    def finish(s, phase):
        axis = ORDERS[s][phase]
        for n, by in enumerate(steps):
            ref = region(s, phase, turn(at[axis], -by), slice(None))
            arrive(ref, send_ag.at[s, phase * 3 + n], recv_ag.at[s, phase * 3 + n], peer(axis, by))

    def last_spread(s):
        axis = ORDERS[s][2]
        for turn_of in range(2):
            for way, by in enumerate((1, -1)):
                n = 6 + way * 2 + turn_of
                mine = region(s, 2, at[axis], way ^ turn_of)
                send(mine, mine, send_ag.at[s, n], recv_ag.at[s, n], peer(axis, by))

    def last_forward(s):
        axis = ORDERS[s][2]
        for way, by in enumerate((1, -1)):
            n = 6 + way * 2
            passed = region(s, 2, turn(at[axis], -by), way)
            arrive(passed, send_ag.at[s, n], recv_ag.at[s, n], peer(axis, by))
            send(passed, passed, send_ag.at[s, 10 + way], recv_ag.at[s, 10 + way], peer(axis, by))

    def last_rest(s):
        axis = ORDERS[s][2]
        for way, by in enumerate((1, -1)):
            n = 7 + way * 2
            arrive(region(s, 2, turn(at[axis], -by), 1 - way), send_ag.at[s, n], recv_ag.at[s, n], peer(axis, by))

    def last_finish(s):
        axis = ORDERS[s][2]
        for way, by in enumerate((1, -1)):
            arrive(region(s, 2, turn(at[axis], 2), way), send_ag.at[s, 10 + way], recv_ag.at[s, 10 + way], peer(axis, by))

    def first(s):
        here[s].wait()
        arrive(gathered[s].at[y, 1 - core, z, x], send0.at[s], recv0.at[s], sib)
        spread(s, 0)

    def second(s):
        finish(s, 0)
        spread(s, 1)

    def third(s):
        finish(s, 1)
        last_spread(s)

    def slots_ready(_):
        own_tiles.wait()
        arrive(tiles_sib.at[pl.ds(0, SLOTS)], misc.at[2], misc.at[3], sib)
        arrive(lists_in, misc.at[0], misc.at[1], sib)
        to_scalar = pltpu.make_async_copy(lists_in, lists_sib, misc.at[5])
        to_scalar.start()
        to_scalar.wait()

    def products(k, group):
        which, tile_ref = ((lists, tiles_own), (lists_sib, tiles_sib))[group]
        per = SUBS // CHUNKS
        parts = slices[k * per : (k + 1) * per]

        def step(q, carry):
            left, right = [], []
            for g in range(GROUP):
                left.append(tile_ref[which[g, q]])
                m = which[GROUP + g, q]
                right.append(jnp.concatenate([ref[m] for ref in parts], axis=1))
            new = jnp.dot(
                jnp.concatenate(left, axis=1), jnp.concatenate(right, axis=0), preferred_element_type=jnp.float32
            )
            history[q + 1] = history[which[0, 64 + q]] + new
            return carry

        lax.fori_loop(0, QUADS, step, 0, unroll=6)
        rows_ref = part.at[k, group].reshape(OUTS * TILE, WIDE)
        for o in range(OUTS):
            rows_ref[o * TILE : (o + 1) * TILE, :] = history[which[1, 64 + o]]

    def block(k, g, b, axis, index):
        return part.at[k, g, b, index] if axis == Z else part.at[k, g, b, :, index]

    def sum_send(k, g):
        axis = SUM_ORDERS[g][0]
        for way, by in enumerate((1, -1)):
            far = block(k, g, way, axis, turn(at[axis], 2))
            send(far, relay.at[k, g, way], send1.at[k, g, way], recv1.at[k, g, way], peer(axis, by))
        for way, by in enumerate((1, -1)):
            near = block(k, g, 1 - way, axis, turn(at[axis], by))
            send(near, got1.at[k, g, way, 1 - way], send1.at[k, g, 2 + way], recv1.at[k, g, 2 + way], peer(axis, by))

    def sum_relay(k, g):
        axis = SUM_ORDERS[g][0]
        for way, by in enumerate((1, -1)):
            arrive(relay.at[k, g, way], send1.at[k, g, way], recv1.at[k, g, way], peer(axis, by))
            index = turn(at[axis], by)
            for i in range(RING):
                own = part[k, g, way, index, i] if axis == Z else part[k, g, way, i, index]
                relay[k, g, way, i] = relay[k, g, way, i] + own
            send(relay.at[k, g, way], got1.at[k, g, way, way], send1.at[k, g, 4 + way], recv1.at[k, g, 4 + way], peer(axis, by))

    def sum_pass(k, g):
        axis, then = SUM_ORDERS[g]
        for way, by in enumerate((1, -1)):
            for n, b in ((2, 1 - way), (4, way)):
                arrive(got1.at[k, g, way, b], send1.at[k, g, n + way], recv1.at[k, g, n + way], peer(axis, by))
        for b in range(NB):
            for i in range(RING):
                own = part[k, g, b, at[Z], i] if axis == Z else part[k, g, b, i, at[X]]
                sum1[k, g, b, i] = own + (got1[k, g, 0, b, i] + got1[k, g, 1, b, i])
        for n, by in enumerate(steps):
            src = sum1.at[k, g, :, turn(at[then], by)]
            send(src, got2.at[k, g, n], send2.at[k, g, n], recv2.at[k, g, n], peer(then, by))

    def sum_end(k, g):
        then = SUM_ORDERS[g][1]
        for n, by in enumerate(steps):
            arrive(got2.at[k, g, n], send2.at[k, g, n], recv2.at[k, g, n], peer(then, by))
        for b in range(NB):
            total = (sum1[k, g, b, at[then]] + got2[k, g, 0, b]) + (got2[k, g, 1, b] + got2[k, g, 2, b])
            if g == 1:
                cross_out[k, b] = total
            else:
                columns = pl.ds(pl.multiple_of(core * (SUBS * LANES) + k * WIDE, WIDE), WIDE)
                owned[b, :, columns] = total
        if g == 1:
            send(cross_out.at[k], cross_in.at[k], send_x.at[k], recv_x.at[k], sib)

    def sum_cross(k):
        arrive(cross_in.at[k], send_x.at[k], recv_x.at[k], sib)
        for b in range(NB):
            columns = pl.ds(pl.multiple_of((1 - core) * (SUBS * LANES) + k * WIDE, WIDE), WIDE)
            owned[b, :, columns] = cross_in[k, b]

    def unit(work):
        return lambda n: work(n // 2, n % 2)

    fwd, rest, done = last_forward, last_rest, last_finish
    mul, out, mid, add, end = (unit(w) for w in (products, sum_send, sum_relay, sum_pass, sum_end))
    plan = [(first, s) for s in range(SUBS)]
    plan += [(second, s) for s in (0, 1, 3, 2)] + [(third, s) for s in (0, 1, 3)]
    plan += [(second, s) for s in (4, 5, 6, 7)] + [(slots_ready, 0)]
    plan += [(fwd, 0), (fwd, 1), (fwd, 3), (rest, 0), (third, 2), (rest, 1), (third, 4), (rest, 3), (third, 5)]
    plan += [(done, 0), (done, 1), (mul, 0), (out, 0)]
    plan += [(fwd, 2), (mul, 1), (out, 1), (mid, 0)]
    plan += [(rest, 2), (third, 6), (fwd, 4), (fwd, 5), (done, 2), (done, 3), (mul, 2), (out, 2), (mid, 1), (add, 0)]
    plan += [(third, 7), (mul, 3), (out, 3), (mid, 2), (add, 1), (fwd, 6)]
    plan += [(rest, 4), (rest, 5), (done, 4), (done, 5), (mul, 4), (out, 4), (mid, 3), (add, 2), (end, 0), (fwd, 7)]
    plan += [(mul, 5), (out, 5), (mid, 4), (add, 3), (end, 1)]
    plan += [(rest, 6), (rest, 7), (done, 6), (done, 7), (mul, 6), (out, 6), (mid, 5), (add, 4), (end, 2)]
    plan += [(mul, 7), (out, 7), (mid, 6), (add, 5), (end, 3), (mid, 7), (add, 6), (end, 4), (end, 5), (add, 7), (end, 6), (end, 7)]
    for work, which in plan:
        work(which)
    for k in range(CHUNKS):
        sum_cross(k)
    for copy in sent:
        copy.wait_send()


def owned_ladder(lists, amplitudes, tiles):
    dma = pltpu.SemaphoreType.DMA
    vmem = pltpu.VMEM
    f32 = jnp.float32
    scratch = [vmem((2 * NT, TILE, LANES), jnp.bfloat16) for _ in range(SUBS)]
    scratch += [
        vmem((SLOTS + 1, TILE, TILE), jnp.bfloat16),
        vmem((SLOTS + 1, TILE, TILE), jnp.bfloat16),
        vmem((QUADS + 1, TILE, WIDE), f32),
        vmem((CHUNKS, 2, NB, RING, RING, OWN, WIDE), f32),
        vmem((CHUNKS, 2, 2, RING, OWN, WIDE), f32),
        vmem((CHUNKS, 2, 2, NB, RING, OWN, WIDE), f32),
        vmem((CHUNKS, 2, NB, RING, OWN, WIDE), f32),
        vmem((CHUNKS, 2, 3, NB, OWN, WIDE), f32),
        vmem((CHUNKS, NB, OWN, WIDE), f32),
        vmem((CHUNKS, NB, OWN, WIDE), f32),
        vmem((8, 128), jnp.int32),
        pltpu.SMEM((8, 128), jnp.int32),
        dma((SUBS,)), dma((SUBS,)), dma((SUBS,)),
        dma((SUBS, 12)), dma((SUBS, 12)),
        dma((CHUNKS, 2, 6)), dma((CHUNKS, 2, 6)), dma((CHUNKS, 2, 3)), dma((CHUNKS, 2, 3)),
        dma((CHUNKS,)), dma((CHUNKS,)), dma((6,)),
    ]
    return pl.pallas_call(
        ladder_kernel,
        out_shape=jax.ShapeDtypeStruct((NB, OWN, 2 * SUBS * LANES), f32),
        in_specs=[
            pl.BlockSpec(memory_space=pltpu.SMEM),
            pl.BlockSpec(memory_space=pl.ANY),
            pl.BlockSpec(memory_space=pl.ANY),
            pl.BlockSpec(memory_space=pl.ANY),
        ],
        out_specs=pl.BlockSpec(memory_space=pltpu.VMEM),
        scratch_shapes=scratch,
        compiler_params=pltpu.CompilerParams(
            collective_id=0, has_side_effects=True, vmem_limit_bytes=60 * 1024 * 1024
        ),
        name="ladder",
    )(lists, lists, amplitudes, tiles)


def per_device(amplitudes, integrals, slot_index, virt_energy, b_energy, pair_energy):
    index = slot_index.reshape(-1, 2)
    tiles = integrals.reshape(-1, TILE, TILE)
    lists = slot_lists(index[:, 0], index[:, 1])
    owned = owned_ladder(lists, amplitudes, tiles)
    denom = virt_energy[None, :, None] + b_energy[:, None, None] - pair_energy[None, None, :]
    return owned / denom


def solution(mesh):
    placed = (
        P(("row", "col"), None),
        P(("row", "col"), None, None, None, None),
        P(("row", "col"), None, None, None),
        P(("row", "col")),
        P(),
        P(),
    )
    return jax.shard_map(
        per_device,
        mesh=mesh,
        in_specs=placed,
        out_specs=P(None, ("row", "col"), None),
        check_vma=False,
    )
```

```python
import functools

import jax
import jax.numpy as jnp
from jax import lax
from jax.experimental import pallas as pl
from jax.experimental.pallas import tpu as pltpu
from jax.sharding import PartitionSpec as P

MESH = pl.DeviceIdType.MESH
NT = 24
NB = 2
TILE = 128
SLOTS = 128
OUTS = 6
GROUP = 4
QUADS = 36
LANES = 128
SUBS = 8
CHUNKS = 4
WIDE = LANES * SUBS // CHUNKS
OWN = 24
ROWS = 48
RING = 4
Y, Z, X = 0, 1, 2
ORDERS = (
    (X, Z, Y), (Z, Y, X),
    (Z, X, Y), (X, Y, Z),
    (Y, Z, X), (Y, X, Z),
    (X, Z, Y), (Z, X, Y),
)
SUM_ORDERS = ((X, Z), (Z, X))


def slot_lists(named):
    i32 = jnp.int32
    square = (SLOTS, SLOTS)
    down, along = lax.broadcasted_iota(i32, square, 0), lax.broadcasted_iota(i32, square, 1)
    out_along = jnp.broadcast_to(named[0:1, :], square)
    out_down, amp_down = out_along.T, jnp.broadcast_to(named[1:2, :], square).T
    same_before = jnp.where((out_along == out_down) & (along < down), 1, 0)
    rank = jnp.sum(same_before, axis=1, keepdims=True)
    start = jnp.zeros((1, SLOTS), i32)
    place = jnp.full(square, -1, i32)
    lane = along[0:1, :]
    came_from, ends = lane, jnp.zeros((1, SLOTS), i32)
    for o in range(OUTS):
        count = jnp.sum(jnp.where(out_down == o, 1, 0), axis=0, keepdims=True)
        quads = (count + (GROUP - 1)) >> 2
        place = jnp.where(out_down == o, start * GROUP + rank, place)
        came_from = jnp.where((lane == start) & (count > 0), 0, came_from)
        start = start + quads
        ends = jnp.where((lane == o) & (count > 0), start, ends)
    tiles, amps = [], []
    for g in range(GROUP):
        here = place == along * GROUP + g
        tiles.append(SLOTS + jnp.sum(jnp.where(here, down - SLOTS, 0), axis=0, keepdims=True))
        amps.append(jnp.sum(jnp.where(here, amp_down, 0), axis=0, keepdims=True))
    return tiles + amps + [came_from, ends]


def ladder_kernel(named, amps, tiles, owned, *scratch):
    slices = scratch[:SUBS]
    gathered = [ref.reshape(4, 2, 4, 4, ROWS, LANES) for ref in slices]
    (tiles_own, tiles_sib, history, part, relay, got1, sum1, got2, cross_out, cross_in, lists_out, lists_in, lists, lists_sib,
     send0, recv0, local0, send_ag, recv_ag, send1, recv1, send2, recv2, send_x, recv_x, misc) = scratch[SUBS:]
    row, col = lax.axis_index("row"), lax.axis_index("col")
    y, core = lax.div(row, 2), lax.rem(row, 2)
    z, x = lax.div(col, RING), lax.rem(col, RING)
    at = (y, z, x)
    sib = (y * 2 + 1 - core, col)

    def turn(value, by):
        return lax.rem(value + by + RING, RING)

    def peer(axis, by):
        place = list(at)
        place[axis] = turn(at[axis], by)
        return (place[Y] * 2 + core, place[Z] * RING + place[X])

    partners = [peer(a, d) for a in (Y, Z, X) for d in (1, -1)] + [peer(a, 2) for a in (Y, Z, X)] + [sib]
    barrier = pltpu.get_barrier_semaphore()
    for partner in partners:
        pl.semaphore_signal(barrier, inc=1, device_id=partner, device_id_type=MESH)
    pl.semaphore_wait(barrier, len(partners))

    sent = []

    def send(src, dst, s_sem, r_sem, to):
        copy = pltpu.make_async_remote_copy(
            src_ref=src, dst_ref=dst, send_sem=s_sem, recv_sem=r_sem, device_id=to, device_id_type=MESH
        )
        copy.start()
        sent.append(copy)

    def arrive(dst, s_sem, r_sem, to):
        pltpu.make_async_remote_copy(
            src_ref=dst, dst_ref=dst, send_sem=s_sem, recv_sem=r_sem, device_id=to, device_id_type=MESH
        ).wait_recv()

    here = []
    for s in range(SUBS):
        mine = pl.ds(pl.multiple_of(core * (SUBS * LANES) + s * LANES, LANES), LANES)
        other = pl.ds(pl.multiple_of((1 - core) * (SUBS * LANES) + s * LANES, LANES), LANES)
        home = gathered[s].at[y, core, z, x]
        send(amps.at[:, other], home, send0.at[s], recv0.at[s], sib)
        copy = pltpu.make_async_copy(amps.at[:, mine], home, local0.at[s])
        copy.start()
        here.append(copy)
    send(tiles, tiles_sib.at[pl.ds(0, SLOTS)], misc.at[2], misc.at[3], sib)
    own_tiles = pltpu.make_async_copy(tiles, tiles_own.at[pl.ds(0, SLOTS)], misc.at[4])
    own_tiles.start()
    for ref in (tiles_own, tiles_sib):
        ref[SLOTS] = jnp.zeros((TILE, TILE), ref.dtype)
    history[0] = jnp.zeros((TILE, WIDE), jnp.float32)

    def region(s, phase, index, half):
        axis = ORDERS[s][phase]
        done = ORDERS[s][:phase]
        pick = [slice(None) if a in done else at[a] for a in (Y, Z, X)]
        pick[axis] = index
        return gathered[s].at[pick[Y], half, pick[Z], pick[X]]

    steps = (1, -1, 2)

    def spread(s, phase):
        axis = ORDERS[s][phase]
        mine = region(s, phase, at[axis], slice(None))
        for n, by in enumerate(steps):
            send(mine, mine, send_ag.at[s, phase * 3 + n], recv_ag.at[s, phase * 3 + n], peer(axis, by))

    def finish(s, phase):
        axis = ORDERS[s][phase]
        for n, by in enumerate(steps):
            ref = region(s, phase, turn(at[axis], -by), slice(None))
            arrive(ref, send_ag.at[s, phase * 3 + n], recv_ag.at[s, phase * 3 + n], peer(axis, by))

    def last_spread(s):
        axis = ORDERS[s][2]
        for turn_of in range(2):
            for way, by in enumerate((1, -1)):
                n = 6 + way * 2 + turn_of
                mine = region(s, 2, at[axis], way ^ turn_of)
                send(mine, mine, send_ag.at[s, n], recv_ag.at[s, n], peer(axis, by))

    def last_forward(s):
        axis = ORDERS[s][2]
        for way, by in enumerate((1, -1)):
            n = 6 + way * 2
            passed = region(s, 2, turn(at[axis], -by), way)
            arrive(passed, send_ag.at[s, n], recv_ag.at[s, n], peer(axis, by))
            send(passed, passed, send_ag.at[s, 10 + way], recv_ag.at[s, 10 + way], peer(axis, by))

    def last_rest(s):
        axis = ORDERS[s][2]
        for way, by in enumerate((1, -1)):
            n = 7 + way * 2
            arrive(region(s, 2, turn(at[axis], -by), 1 - way), send_ag.at[s, n], recv_ag.at[s, n], peer(axis, by))

    def last_finish(s):
        axis = ORDERS[s][2]
        for way, by in enumerate((1, -1)):
            arrive(region(s, 2, turn(at[axis], 2), way), send_ag.at[s, 10 + way], recv_ag.at[s, 10 + way], peer(axis, by))

    def first(s):
        here[s].wait()
        arrive(gathered[s].at[y, 1 - core, z, x], send0.at[s], recv0.at[s], sib)
        spread(s, 0)

    def second(s):
        finish(s, 0)
        spread(s, 1)

    def third(s):
        finish(s, 1)
        last_spread(s)

    def slots_sent(_):
        for n, row_of in enumerate(slot_lists(named[...])):
            lists_out[n : n + 1, :] = row_of
        for n in range(10, 16):
            lists_out[n : n + 1, :] = jnp.zeros((1, SLOTS), jnp.int32)
        send(lists_out, lists_in, misc.at[0], misc.at[1], sib)
        to_scalar = pltpu.make_async_copy(lists_out, lists, misc.at[6])
        to_scalar.start()
        to_scalar.wait()

    def slots_ready(_):
        own_tiles.wait()
        arrive(tiles_sib.at[pl.ds(0, SLOTS)], misc.at[2], misc.at[3], sib)
        arrive(lists_in, misc.at[0], misc.at[1], sib)
        to_scalar = pltpu.make_async_copy(lists_in, lists_sib, misc.at[5])
        to_scalar.start()
        to_scalar.wait()

    def products(k, group):
        which, tile_ref = ((lists, tiles_own), (lists_sib, tiles_sib))[group]
        per = SUBS // CHUNKS
        parts = slices[k * per : (k + 1) * per]

        def step(q, carry):
            left, right = [], []
            for g in range(GROUP):
                left.append(tile_ref[which[g, q]])
                m = which[GROUP + g, q]
                right.append(jnp.concatenate([ref[m] for ref in parts], axis=1))
            new = jnp.dot(
                jnp.concatenate(left, axis=1), jnp.concatenate(right, axis=0), preferred_element_type=jnp.float32
            )
            history[q + 1] = history[which[8, q]] + new
            return carry

        lax.fori_loop(0, QUADS, step, 0, unroll=12)
        rows_ref = part.at[k, group].reshape(OUTS * TILE, WIDE)
        for o in range(OUTS):
            rows_ref[o * TILE : (o + 1) * TILE, :] = history[which[9, o]]

    def block(k, g, b, axis, index):
        return part.at[k, g, b, index] if axis == Z else part.at[k, g, b, :, index]

    def sum_send(k, g):
        axis = SUM_ORDERS[g][0]
        for way, by in enumerate((1, -1)):
            far = block(k, g, way, axis, turn(at[axis], 2))
            send(far, relay.at[k, g, way], send1.at[k, g, way], recv1.at[k, g, way], peer(axis, by))
        for way, by in enumerate((1, -1)):
            near = block(k, g, 1 - way, axis, turn(at[axis], by))
            send(near, got1.at[k, g, way, 1 - way], send1.at[k, g, 2 + way], recv1.at[k, g, 2 + way], peer(axis, by))

    def sum_relay(k, g):
        axis = SUM_ORDERS[g][0]
        for way, by in enumerate((1, -1)):
            arrive(relay.at[k, g, way], send1.at[k, g, way], recv1.at[k, g, way], peer(axis, by))
            index = turn(at[axis], by)
            for i in range(RING):
                own = part[k, g, way, index, i] if axis == Z else part[k, g, way, i, index]
                relay[k, g, way, i] = relay[k, g, way, i] + own
            send(relay.at[k, g, way], got1.at[k, g, way, way], send1.at[k, g, 4 + way], recv1.at[k, g, 4 + way], peer(axis, by))

    def sum_pass(k, g):
        axis, then = SUM_ORDERS[g]
        for way, by in enumerate((1, -1)):
            for n, b in ((2, 1 - way), (4, way)):
                arrive(got1.at[k, g, way, b], send1.at[k, g, n + way], recv1.at[k, g, n + way], peer(axis, by))
        for b in range(NB):
            for i in range(RING):
                own = part[k, g, b, at[Z], i] if axis == Z else part[k, g, b, i, at[X]]
                sum1[k, g, b, i] = own + (got1[k, g, 0, b, i] + got1[k, g, 1, b, i])
        for n, by in enumerate(steps):
            src = sum1.at[k, g, :, turn(at[then], by)]
            send(src, got2.at[k, g, n], send2.at[k, g, n], recv2.at[k, g, n], peer(then, by))

    def sum_end(k, g):
        then = SUM_ORDERS[g][1]
        for n, by in enumerate(steps):
            arrive(got2.at[k, g, n], send2.at[k, g, n], recv2.at[k, g, n], peer(then, by))
        for b in range(NB):
            total = (sum1[k, g, b, at[then]] + got2[k, g, 0, b]) + (got2[k, g, 1, b] + got2[k, g, 2, b])
            if g == 1:
                cross_out[k, b] = total
            else:
                columns = pl.ds(pl.multiple_of(core * (SUBS * LANES) + k * WIDE, WIDE), WIDE)
                owned[b, :, columns] = total
        if g == 1:
            send(cross_out.at[k], cross_in.at[k], send_x.at[k], recv_x.at[k], sib)

    def sum_cross(k):
        arrive(cross_in.at[k], send_x.at[k], recv_x.at[k], sib)
        for b in range(NB):
            columns = pl.ds(pl.multiple_of((1 - core) * (SUBS * LANES) + k * WIDE, WIDE), WIDE)
            owned[b, :, columns] = cross_in[k, b]

    def unit(work):
        return lambda n: work(n // 2, n % 2)

    fwd, rest, done = last_forward, last_rest, last_finish
    mul, out, mid, add, end = (unit(w) for w in (products, sum_send, sum_relay, sum_pass, sum_end))
    plan = [(first, s) for s in (0, 1, 3, 2)] + [(slots_sent, 0)] + [(second, s) for s in (0, 1, 3, 2)]
    plan += [(first, s) for s in (4, 5, 6, 7)] + [(third, s) for s in (0, 1, 3)]
    plan += [(second, s) for s in (6, 7, 4, 5)] + [(slots_ready, 0)]
    plan += [(fwd, 0), (fwd, 1), (fwd, 3), (rest, 0), (third, 2), (rest, 1), (third, 4), (rest, 3), (third, 5)]
    plan += [(done, 0), (done, 1), (mul, 0), (out, 0)]
    plan += [(fwd, 2), (mul, 1), (out, 1), (mid, 0)]
    plan += [(rest, 2), (third, 6), (fwd, 4), (fwd, 5), (done, 2), (done, 3), (mul, 2), (out, 2), (mid, 1), (add, 0)]
    plan += [(third, 7), (mul, 3), (out, 3), (mid, 2), (add, 1), (fwd, 6)]
    plan += [(rest, 4), (rest, 5), (done, 4), (done, 5), (mul, 4), (out, 4), (mid, 3), (add, 2), (end, 0), (fwd, 7)]
    plan += [(mul, 5), (out, 5), (mid, 4), (add, 3), (end, 1)]
    plan += [(rest, 6), (rest, 7), (done, 6), (done, 7), (mul, 6), (out, 6), (mid, 5), (add, 4), (end, 2)]
    plan += [(mul, 7), (out, 7), (mid, 6), (add, 5), (end, 3), (mid, 7), (add, 6), (end, 4), (end, 5), (add, 7), (end, 6), (end, 7)]
    for work, which in plan:
        work(which)
    for k in range(CHUNKS):
        sum_cross(k)
    for copy in sent:
        copy.wait_send()


def owned_ladder(named, amplitudes, tiles):
    dma = pltpu.SemaphoreType.DMA
    vmem = pltpu.VMEM
    f32 = jnp.float32
    scratch = [vmem((2 * NT, TILE, LANES), jnp.bfloat16) for _ in range(SUBS)]
    scratch += [
        vmem((SLOTS + 1, TILE, TILE), jnp.bfloat16),
        vmem((SLOTS + 1, TILE, TILE), jnp.bfloat16),
        vmem((QUADS + 1, TILE, WIDE), f32),
        vmem((CHUNKS, 2, NB, RING, RING, OWN, WIDE), f32),
        vmem((CHUNKS, 2, 2, RING, OWN, WIDE), f32),
        vmem((CHUNKS, 2, 2, NB, RING, OWN, WIDE), f32),
        vmem((CHUNKS, 2, NB, RING, OWN, WIDE), f32),
        vmem((CHUNKS, 2, 3, NB, OWN, WIDE), f32),
        vmem((CHUNKS, NB, OWN, WIDE), f32),
        vmem((CHUNKS, NB, OWN, WIDE), f32),
        vmem((16, 128), jnp.int32),
        vmem((16, 128), jnp.int32),
        pltpu.SMEM((16, 128), jnp.int32),
        pltpu.SMEM((16, 128), jnp.int32),
        dma((SUBS,)), dma((SUBS,)), dma((SUBS,)),
        dma((SUBS, 12)), dma((SUBS, 12)),
        dma((CHUNKS, 2, 6)), dma((CHUNKS, 2, 6)), dma((CHUNKS, 2, 3)), dma((CHUNKS, 2, 3)),
        dma((CHUNKS,)), dma((CHUNKS,)), dma((8,)),
    ]
    return pl.pallas_call(
        ladder_kernel,
        out_shape=jax.ShapeDtypeStruct((NB, OWN, 2 * SUBS * LANES), f32),
        in_specs=[
            pl.BlockSpec(memory_space=pltpu.VMEM),
            pl.BlockSpec(memory_space=pl.ANY),
            pl.BlockSpec(memory_space=pl.ANY),
        ],
        out_specs=pl.BlockSpec(memory_space=pltpu.VMEM),
        scratch_shapes=scratch,
        compiler_params=pltpu.CompilerParams(
            collective_id=0, has_side_effects=True, vmem_limit_bytes=60 * 1024 * 1024
        ),
        name="ladder",
    )(named, amplitudes, tiles)


def per_device(amplitudes, integrals, slot_index, virt_energy, b_energy, pair_energy):
    named = slot_index.reshape(-1, 2).T
    tiles = integrals.reshape(-1, TILE, TILE)
    owned = owned_ladder(named, amplitudes, tiles)
    denom = virt_energy[None, :, None] + b_energy[:, None, None] - pair_energy[None, None, :]
    return owned / denom


def solution(mesh):
    placed = (
        P(("row", "col"), None),
        P(("row", "col"), None, None, None, None),
        P(("row", "col"), None, None, None),
        P(("row", "col")),
        P(),
        P(),
    )
    return jax.shard_map(
        per_device,
        mesh=mesh,
        in_specs=placed,
        out_specs=P(None, ("row", "col"), None),
        check_vma=False,
    )
```

```python
import functools

import jax
import jax.numpy as jnp
from jax import lax
from jax.experimental import pallas as pl
from jax.experimental.pallas import tpu as pltpu
from jax.sharding import PartitionSpec as P

MESH = pl.DeviceIdType.MESH
NT = 24
NB = 2
TILE = 128
SLOTS = 128
CAP = 8
OUTS = 6
GROUP = 4
QUADS = 36
LANES = 128
SUBS = 8
CHUNKS = 4
WIDE = LANES * SUBS // CHUNKS
OWN = 24
ROWS = 48
RING = 4
Y, Z, X = 0, 1, 2
ORDERS = (
    (X, Z, Y), (Z, Y, X),
    (Z, X, Y), (X, Y, Z),
    (Y, Z, X), (Y, X, Z),
    (X, Z, Y), (Z, X, Y),
)
SUM_ORDERS = ((X, Z), (Z, X))


def slot_lists(named):
    i32 = jnp.int32
    square = (SLOTS, SLOTS)
    down, along = lax.broadcasted_iota(i32, square, 0), lax.broadcasted_iota(i32, square, 1)
    out_of, amp_of = (jnp.concatenate([named[t, n : n + 1, :] for t in range(CAP)], axis=1) for n in range(2))
    out_along = jnp.broadcast_to(out_of, square)
    out_down, amp_down = out_along.T, jnp.broadcast_to(amp_of, square).T
    tile_down = ((down & 15) << 3) + (down >> 4)
    same_before = jnp.where((out_along == out_down) & (along < down), 1, 0)
    rank = jnp.sum(same_before, axis=1, keepdims=True)
    start = jnp.zeros((1, SLOTS), i32)
    place = jnp.full(square, -1, i32)
    lane = along[0:1, :]
    came_from, ends = lane, jnp.zeros((1, SLOTS), i32)
    for o in range(OUTS):
        count = jnp.sum(jnp.where(out_down == o, 1, 0), axis=0, keepdims=True)
        quads = (count + (GROUP - 1)) >> 2
        place = jnp.where(out_down == o, start * GROUP + rank, place)
        came_from = jnp.where((lane == start) & (count > 0), 0, came_from)
        start = start + quads
        ends = jnp.where((lane == o) & (count > 0), start, ends)
    tiles, amps = [], []
    for g in range(GROUP):
        here = place == along * GROUP + g
        tiles.append(SLOTS + jnp.sum(jnp.where(here, tile_down - SLOTS, 0), axis=0, keepdims=True))
        amps.append(jnp.sum(jnp.where(here, amp_down, 0), axis=0, keepdims=True))
    return tiles + amps + [came_from, ends]


def ladder_kernel(named, virt, b_level, pair, amps, tiles, owned, *scratch):
    slices = scratch[:SUBS]
    gathered = [ref.reshape(4, 2, 4, 4, ROWS, LANES) for ref in slices]
    (tiles_own, tiles_sib, history, part, relay, got1, sum1, got2, cross_out, cross_in, lists_out, lists_in, lists, lists_sib,
     send0, recv0, local0, send_ag, recv_ag, send1, recv1, send2, recv2, send_x, recv_x, misc) = scratch[SUBS:]
    row, col = lax.axis_index("row"), lax.axis_index("col")
    y, core = lax.div(row, 2), lax.rem(row, 2)
    z, x = lax.div(col, RING), lax.rem(col, RING)
    at = (y, z, x)
    sib = (y * 2 + 1 - core, col)

    def turn(value, by):
        return lax.rem(value + by + RING, RING)

    def peer(axis, by):
        place = list(at)
        place[axis] = turn(at[axis], by)
        return (place[Y] * 2 + core, place[Z] * RING + place[X])

    square = (OWN, OWN)
    diagonal = lax.broadcasted_iota(jnp.int32, square, 0) == lax.broadcasted_iota(jnp.int32, square, 1)
    virt_down = jnp.sum(jnp.where(diagonal, jnp.broadcast_to(virt[...], square), 0.0), axis=1, keepdims=True)

    def divided(total, b, columns):
        return total / (virt_down + b_level[b] - pair[:, columns])

    partners = [peer(a, d) for a in (Y, Z, X) for d in (1, -1)] + [peer(a, 2) for a in (Y, Z, X)] + [sib]
    barrier = pltpu.get_barrier_semaphore()
    for partner in partners:
        pl.semaphore_signal(barrier, inc=1, device_id=partner, device_id_type=MESH)
    pl.semaphore_wait(barrier, len(partners))

    sent = []

    def send(src, dst, s_sem, r_sem, to):
        copy = pltpu.make_async_remote_copy(
            src_ref=src, dst_ref=dst, send_sem=s_sem, recv_sem=r_sem, device_id=to, device_id_type=MESH
        )
        copy.start()
        sent.append(copy)

    def arrive(dst, s_sem, r_sem, to):
        pltpu.make_async_remote_copy(
            src_ref=dst, dst_ref=dst, send_sem=s_sem, recv_sem=r_sem, device_id=to, device_id_type=MESH
        ).wait_recv()

    here = []
    for s in range(SUBS):
        mine = pl.ds(pl.multiple_of(core * (SUBS * LANES) + s * LANES, LANES), LANES)
        other = pl.ds(pl.multiple_of((1 - core) * (SUBS * LANES) + s * LANES, LANES), LANES)
        home = gathered[s].at[y, core, z, x]
        send(amps.at[:, other], home, send0.at[s], recv0.at[s], sib)
        copy = pltpu.make_async_copy(amps.at[:, mine], home, local0.at[s])
        copy.start()
        here.append(copy)
    send(tiles, tiles_sib.at[pl.ds(0, SLOTS)], misc.at[2], misc.at[3], sib)
    own_tiles = pltpu.make_async_copy(tiles, tiles_own.at[pl.ds(0, SLOTS)], misc.at[4])
    own_tiles.start()
    for ref in (tiles_own, tiles_sib):
        ref[SLOTS] = jnp.zeros((TILE, TILE), ref.dtype)
    history[0] = jnp.zeros((TILE, WIDE), jnp.float32)

    def region(s, phase, index, half):
        axis = ORDERS[s][phase]
        done = ORDERS[s][:phase]
        pick = [slice(None) if a in done else at[a] for a in (Y, Z, X)]
        pick[axis] = index
        return gathered[s].at[pick[Y], half, pick[Z], pick[X]]

    steps = (1, -1, 2)

    def spread(s, phase):
        axis = ORDERS[s][phase]
        mine = region(s, phase, at[axis], slice(None))
        for n, by in enumerate(steps):
            send(mine, mine, send_ag.at[s, phase * 3 + n], recv_ag.at[s, phase * 3 + n], peer(axis, by))

    def finish(s, phase):
        axis = ORDERS[s][phase]
        for n, by in enumerate(steps):
            ref = region(s, phase, turn(at[axis], -by), slice(None))
            arrive(ref, send_ag.at[s, phase * 3 + n], recv_ag.at[s, phase * 3 + n], peer(axis, by))

    def last_spread(s):
        axis = ORDERS[s][2]
        for turn_of in range(2):
            for way, by in enumerate((1, -1)):
                n = 6 + way * 2 + turn_of
                mine = region(s, 2, at[axis], way ^ turn_of)
                send(mine, mine, send_ag.at[s, n], recv_ag.at[s, n], peer(axis, by))

    def last_forward(s):
        axis = ORDERS[s][2]
        for way, by in enumerate((1, -1)):
            n = 6 + way * 2
            passed = region(s, 2, turn(at[axis], -by), way)
            arrive(passed, send_ag.at[s, n], recv_ag.at[s, n], peer(axis, by))
            send(passed, passed, send_ag.at[s, 10 + way], recv_ag.at[s, 10 + way], peer(axis, by))

    def last_rest(s):
        axis = ORDERS[s][2]
        for way, by in enumerate((1, -1)):
            n = 7 + way * 2
            arrive(region(s, 2, turn(at[axis], -by), 1 - way), send_ag.at[s, n], recv_ag.at[s, n], peer(axis, by))

    def last_finish(s):
        axis = ORDERS[s][2]
        for way, by in enumerate((1, -1)):
            arrive(region(s, 2, turn(at[axis], 2), way), send_ag.at[s, 10 + way], recv_ag.at[s, 10 + way], peer(axis, by))

    def first(s):
        here[s].wait()
        arrive(gathered[s].at[y, 1 - core, z, x], send0.at[s], recv0.at[s], sib)
        spread(s, 0)

    def second(s):
        finish(s, 0)
        spread(s, 1)

    def third(s):
        finish(s, 1)
        last_spread(s)

    def slots_sent(_):
        for n, row_of in enumerate(slot_lists(named[...])):
            lists_out[n : n + 1, :] = row_of
        for n in range(10, 16):
            lists_out[n : n + 1, :] = jnp.zeros((1, SLOTS), jnp.int32)
        send(lists_out, lists_in, misc.at[0], misc.at[1], sib)
        to_scalar = pltpu.make_async_copy(lists_out, lists, misc.at[6])
        to_scalar.start()
        to_scalar.wait()

    def slots_ready(_):
        own_tiles.wait()
        arrive(tiles_sib.at[pl.ds(0, SLOTS)], misc.at[2], misc.at[3], sib)
        arrive(lists_in, misc.at[0], misc.at[1], sib)
        to_scalar = pltpu.make_async_copy(lists_in, lists_sib, misc.at[5])
        to_scalar.start()
        to_scalar.wait()

    def products(k, group):
        which, tile_ref = ((lists, tiles_own), (lists_sib, tiles_sib))[group]
        per = SUBS // CHUNKS
        parts = slices[k * per : (k + 1) * per]

        def step(q, carry):
            left, right = [], []
            for g in range(GROUP):
                left.append(tile_ref[which[g, q]])
                m = which[GROUP + g, q]
                right.append(jnp.concatenate([ref[m] for ref in parts], axis=1))
            new = jnp.dot(
                jnp.concatenate(left, axis=1), jnp.concatenate(right, axis=0), preferred_element_type=jnp.float32
            )
            history[q + 1] = history[which[8, q]] + new
            return carry

        lax.fori_loop(0, QUADS, step, 0, unroll=12)
        rows_ref = part.at[k, group].reshape(OUTS * TILE, WIDE)
        for o in range(OUTS):
            rows_ref[o * TILE : (o + 1) * TILE, :] = history[which[9, o]]

    def block(k, g, b, axis, index):
        return part.at[k, g, b, index] if axis == Z else part.at[k, g, b, :, index]

    def sum_send(k, g):
        axis = SUM_ORDERS[g][0]
        for way, by in enumerate((1, -1)):
            far = block(k, g, way, axis, turn(at[axis], 2))
            send(far, relay.at[k, g, way], send1.at[k, g, way], recv1.at[k, g, way], peer(axis, by))
        for way, by in enumerate((1, -1)):
            near = block(k, g, 1 - way, axis, turn(at[axis], by))
            send(near, got1.at[k, g, way, 1 - way], send1.at[k, g, 2 + way], recv1.at[k, g, 2 + way], peer(axis, by))

    def sum_relay(k, g):
        axis = SUM_ORDERS[g][0]
        for way, by in enumerate((1, -1)):
            arrive(relay.at[k, g, way], send1.at[k, g, way], recv1.at[k, g, way], peer(axis, by))
            index = turn(at[axis], by)
            for i in range(RING):
                own = part[k, g, way, index, i] if axis == Z else part[k, g, way, i, index]
                relay[k, g, way, i] = relay[k, g, way, i] + own
            send(relay.at[k, g, way], got1.at[k, g, way, way], send1.at[k, g, 4 + way], recv1.at[k, g, 4 + way], peer(axis, by))

    def sum_pass(k, g):
        axis, then = SUM_ORDERS[g]
        for way, by in enumerate((1, -1)):
            for n, b in ((2, 1 - way), (4, way)):
                arrive(got1.at[k, g, way, b], send1.at[k, g, n + way], recv1.at[k, g, n + way], peer(axis, by))
        for b in range(NB):
            for i in range(RING):
                own = part[k, g, b, at[Z], i] if axis == Z else part[k, g, b, i, at[X]]
                sum1[k, g, b, i] = own + (got1[k, g, 0, b, i] + got1[k, g, 1, b, i])
        for n, by in enumerate(steps):
            src = sum1.at[k, g, :, turn(at[then], by)]
            send(src, got2.at[k, g, n], send2.at[k, g, n], recv2.at[k, g, n], peer(then, by))

    def sum_end(k, g):
        then = SUM_ORDERS[g][1]
        for n, by in enumerate(steps):
            arrive(got2.at[k, g, n], send2.at[k, g, n], recv2.at[k, g, n], peer(then, by))
        for b in range(NB):
            total = (sum1[k, g, b, at[then]] + got2[k, g, 0, b]) + (got2[k, g, 1, b] + got2[k, g, 2, b])
            if g == 1:
                cross_out[k, b] = total
            else:
                columns = pl.ds(pl.multiple_of(core * (SUBS * LANES) + k * WIDE, WIDE), WIDE)
                owned[b, :, columns] = divided(total, b, columns)
        if g == 1:
            send(cross_out.at[k], cross_in.at[k], send_x.at[k], recv_x.at[k], sib)

    def sum_cross(k):
        arrive(cross_in.at[k], send_x.at[k], recv_x.at[k], sib)
        for b in range(NB):
            columns = pl.ds(pl.multiple_of((1 - core) * (SUBS * LANES) + k * WIDE, WIDE), WIDE)
            owned[b, :, columns] = divided(cross_in[k, b], b, columns)

    def unit(work):
        return lambda n: work(n // 2, n % 2)

    fwd, rest, done = last_forward, last_rest, last_finish
    mul, out, mid, add, end = (unit(w) for w in (products, sum_send, sum_relay, sum_pass, sum_end))
    plan = [(first, s) for s in (0, 1, 3, 2)] + [(slots_sent, 0)] + [(second, s) for s in (0, 1, 3, 2)]
    plan += [(first, s) for s in (4, 5, 6, 7)] + [(third, s) for s in (0, 1, 3)]
    plan += [(second, s) for s in (6, 7, 4, 5)] + [(slots_ready, 0)]
    plan += [(fwd, 0), (fwd, 1), (fwd, 3), (rest, 0), (third, 2), (rest, 1), (third, 4), (rest, 3), (third, 5)]
    plan += [(done, 0), (done, 1), (mul, 0), (out, 0)]
    plan += [(fwd, 2), (mul, 1), (out, 1), (mid, 0)]
    plan += [(rest, 2), (third, 6), (fwd, 4), (fwd, 5), (done, 2), (done, 3), (mul, 2), (out, 2), (mid, 1), (add, 0)]
    plan += [(third, 7), (mul, 3), (out, 3), (mid, 2), (add, 1), (fwd, 6)]
    plan += [(rest, 4), (rest, 5), (done, 4), (done, 5), (mul, 4), (out, 4), (mid, 3), (add, 2), (end, 0), (fwd, 7)]
    plan += [(mul, 5), (out, 5), (mid, 4), (add, 3), (end, 1)]
    plan += [(rest, 6), (rest, 7), (done, 6), (done, 7), (mul, 6), (out, 6), (mid, 5), (add, 4), (end, 2)]
    plan += [(mul, 7), (out, 7), (mid, 6), (add, 5), (end, 3), (mid, 7), (add, 6), (end, 4), (end, 5), (add, 7), (end, 6), (end, 7)]
    for work, which in plan:
        work(which)
    for k in range(CHUNKS):
        sum_cross(k)
    for copy in sent:
        copy.wait_send()


def owned_update(named, virt, b_level, pair, amplitudes, tiles):
    dma = pltpu.SemaphoreType.DMA
    vmem = pltpu.VMEM
    f32 = jnp.float32
    scratch = [vmem((2 * NT, TILE, LANES), jnp.bfloat16) for _ in range(SUBS)]
    scratch += [
        vmem((SLOTS + 1, TILE, TILE), jnp.bfloat16),
        vmem((SLOTS + 1, TILE, TILE), jnp.bfloat16),
        vmem((QUADS + 1, TILE, WIDE), f32),
        vmem((CHUNKS, 2, NB, RING, RING, OWN, WIDE), f32),
        vmem((CHUNKS, 2, 2, RING, OWN, WIDE), f32),
        vmem((CHUNKS, 2, 2, NB, RING, OWN, WIDE), f32),
        vmem((CHUNKS, 2, NB, RING, OWN, WIDE), f32),
        vmem((CHUNKS, 2, 3, NB, OWN, WIDE), f32),
        vmem((CHUNKS, NB, OWN, WIDE), f32),
        vmem((CHUNKS, NB, OWN, WIDE), f32),
        vmem((16, 128), jnp.int32),
        vmem((16, 128), jnp.int32),
        pltpu.SMEM((16, 128), jnp.int32),
        pltpu.SMEM((16, 128), jnp.int32),
        dma((SUBS,)), dma((SUBS,)), dma((SUBS,)),
        dma((SUBS, 12)), dma((SUBS, 12)),
        dma((CHUNKS, 2, 6)), dma((CHUNKS, 2, 6)), dma((CHUNKS, 2, 3)), dma((CHUNKS, 2, 3)),
        dma((CHUNKS,)), dma((CHUNKS,)), dma((8,)),
    ]
    return pl.pallas_call(
        ladder_kernel,
        out_shape=jax.ShapeDtypeStruct((NB, OWN, 2 * SUBS * LANES), f32),
        in_specs=[
            pl.BlockSpec(memory_space=pltpu.VMEM),
            pl.BlockSpec(memory_space=pltpu.VMEM),
            pl.BlockSpec(memory_space=pltpu.SMEM),
            pl.BlockSpec(memory_space=pltpu.VMEM),
            pl.BlockSpec(memory_space=pl.ANY),
            pl.BlockSpec(memory_space=pl.ANY),
        ],
        out_specs=pl.BlockSpec(memory_space=pltpu.VMEM),
        scratch_shapes=scratch,
        compiler_params=pltpu.CompilerParams(
            collective_id=0, has_side_effects=True, vmem_limit_bytes=60 * 1024 * 1024
        ),
        name="ladder",
    )(named, virt, b_level, pair, amplitudes, tiles)


def per_device(amplitudes, integrals, slot_index, virt_energy, b_energy, pair_energy):
    named = slot_index[0].transpose(1, 2, 0)
    tiles = integrals.reshape(-1, TILE, TILE)
    return owned_update(named, virt_energy[None, :], b_energy, pair_energy[None, :], amplitudes, tiles)


def solution(mesh):
    placed = (
        P(("row", "col"), None),
        P(("row", "col"), None, None, None, None),
        P(("row", "col"), None, None, None),
        P(("row", "col")),
        P(),
        P(),
    )
    return jax.shard_map(
        per_device,
        mesh=mesh,
        in_specs=placed,
        out_specs=P(None, ("row", "col"), None),
        check_vma=False,
    )
```

```python
import functools

import jax
import jax.numpy as jnp
from jax import lax
from jax.experimental import pallas as pl
from jax.experimental.pallas import tpu as pltpu
from jax.sharding import PartitionSpec as P

MESH = pl.DeviceIdType.MESH
NT = 24
NB = 2
TILE = 128
SLOTS = 128
CAP = 8
OUTS = 6
GROUP = 4
QUADS = 36
LANES = 128
SUBS = 8
CHUNK_SUBS = ((0, 1), (2, 3), (4, 5), (6, 7))
CHUNKS = len(CHUNK_SUBS)
WIDE = 2 * LANES
OWN = 24
STEPS = 32000.0
ROWS = 48
RING = 4
Y, Z, X = 0, 1, 2
ORDERS = (
    (X, Z, Y), (Z, Y, X),
    (Z, X, Y), (X, Y, Z),
    (Y, Z, X), (Y, X, Z),
    (X, Z, Y), (Z, X, Y),
)
AWAY = ((2, 2), (2, 1), (2, 3), (1, 2), (3, 2), (1, 1), (1, 3), (3, 1), (3, 3), (2, 0), (0, 2), (1, 0), (3, 0), (0, 1), (0, 3))
FIRST = (0, 1, 3, 2, 4, 5, 6, 7)
SUM_ORDERS = ((X, Z), (Z, X))


def slot_lists(named):
    i32 = jnp.int32
    square = (SLOTS, SLOTS)
    down, along = lax.broadcasted_iota(i32, square, 0), lax.broadcasted_iota(i32, square, 1)
    out_of, amp_of = (jnp.concatenate([named[t, n : n + 1, :] for t in range(CAP)], axis=1) for n in range(2))
    out_along = jnp.broadcast_to(out_of, square)
    out_down, amp_down = out_along.T, jnp.broadcast_to(amp_of, square).T
    tile_down = ((down & 15) << 3) + (down >> 4)
    same_before = jnp.where((out_along == out_down) & (along < down), 1, 0)
    rank = jnp.sum(same_before, axis=1, keepdims=True)
    start = jnp.zeros((1, SLOTS), i32)
    place = jnp.full(square, -1, i32)
    lane = along[0:1, :]
    came_from, ends = lane, jnp.zeros((1, SLOTS), i32)
    for o in range(OUTS):
        count = jnp.sum(jnp.where(out_down == o, 1, 0), axis=0, keepdims=True)
        quads = (count + (GROUP - 1)) >> 2
        place = jnp.where(out_down == o, start * GROUP + rank, place)
        came_from = jnp.where((lane == start) & (count > 0), 0, came_from)
        start = start + quads
        ends = jnp.where((lane == o) & (count > 0), start, ends)
    tiles, amps = [], []
    for g in range(GROUP):
        here = place == along * GROUP + g
        tiles.append(SLOTS + jnp.sum(jnp.where(here, tile_down - SLOTS, 0), axis=0, keepdims=True))
        amps.append(jnp.sum(jnp.where(here, amp_down, 0), axis=0, keepdims=True))
    return tiles + amps + [came_from, ends]


def encode(ref, values):
    powers = []
    words = len(values) // 2
    for j in range(words):
        whole = []
        for value in values[2 * j : 2 * j + 2]:
            top = jnp.max(jnp.abs(value), axis=0, keepdims=True)
            power = jnp.ceil(jnp.log2(jnp.maximum(top, 1e-30)))
            whole.append(jnp.round(value * (STEPS * jnp.exp2(-power))).astype(jnp.int32))
            powers.append(power)
        ref[j * OWN : (j + 1) * OWN, :] = (whole[1] << 16) | (whole[0] & 0xFFFF)
    while len(powers) < 8:
        powers.append(powers[-1])
    ref[words * OWN : words * OWN + 8, :] = jnp.concatenate(powers, axis=0).astype(jnp.int32)


def decode(ref, blocks):
    words = blocks // 2
    scales = jnp.exp2(ref[words * OWN : words * OWN + 8, :].astype(jnp.float32)) * (1.0 / STEPS)
    values = []
    for j in range(words):
        word = ref[j * OWN : (j + 1) * OWN, :]
        values.append(((word << 16) >> 16).astype(jnp.float32) * scales[2 * j : 2 * j + 1, :])
        values.append((word >> 16).astype(jnp.float32) * scales[2 * j + 1 : 2 * j + 2, :])
    return values


def message(blocks):
    return pl.ds(0, blocks // 2 * OWN + 8)


def ladder_kernel(named, virt, b_level, pair, amps, tiles, owned, *scratch):
    slices = scratch[:SUBS]
    gathered = [ref.reshape(4, 2, 4, 4, ROWS, LANES) for ref in slices]
    (tiles_own, tiles_sib, history, part, far_out, near_out, mid_out, far_in, got1, sum1, next_out, got2, all_out, all_in, cross_out, cross_in, lists_out, lists_in, lists, lists_sib,
     send0, recv0, local0, send_ag, recv_ag, send1, recv1, send2, recv2, send_x, recv_x, send_all, recv_all, misc) = scratch[SUBS:]
    row, col = lax.axis_index("row"), lax.axis_index("col")
    y, core = lax.div(row, 2), lax.rem(row, 2)
    z, x = lax.div(col, RING), lax.rem(col, RING)
    at = (y, z, x)
    sib = (y * 2 + 1 - core, col)

    def turn(value, by):
        return lax.rem(value + by + RING, RING)

    def peer(axis, by):
        place = list(at)
        place[axis] = turn(at[axis], by)
        return (place[Y] * 2 + core, place[Z] * RING + place[X])

    square = (OWN, OWN)
    diagonal = lax.broadcasted_iota(jnp.int32, square, 0) == lax.broadcasted_iota(jnp.int32, square, 1)
    virt_down = jnp.sum(jnp.where(diagonal, jnp.broadcast_to(virt[...], square), 0.0), axis=1, keepdims=True)

    def divided(total, b, columns):
        return total / (virt_down + b_level[b] - pair[:, columns])

    partners = [peer(a, d) for a in (Y, Z, X) for d in (1, -1)] + [peer(a, 2) for a in (Y, Z, X)] + [sib]
    barrier = pltpu.get_barrier_semaphore()
    for partner in partners:
        pl.semaphore_signal(barrier, inc=1, device_id=partner, device_id_type=MESH)
    pl.semaphore_wait(barrier, len(partners))

    sent = []

    def send(src, dst, s_sem, r_sem, to):
        copy = pltpu.make_async_remote_copy(
            src_ref=src, dst_ref=dst, send_sem=s_sem, recv_sem=r_sem, device_id=to, device_id_type=MESH
        )
        copy.start()
        sent.append(copy)

    def arrive(dst, s_sem, r_sem, to):
        pltpu.make_async_remote_copy(
            src_ref=dst, dst_ref=dst, send_sem=s_sem, recv_sem=r_sem, device_id=to, device_id_type=MESH
        ).wait_recv()

    steps = (1, -1, 2)

    here = {}
    for s in FIRST:
        mine = pl.ds(pl.multiple_of(core * (SUBS * LANES) + s * LANES, LANES), LANES)
        other = pl.ds(pl.multiple_of((1 - core) * (SUBS * LANES) + s * LANES, LANES), LANES)
        home = gathered[s].at[y, core, z, x]
        send(amps.at[:, other], home, send0.at[s], recv0.at[s], sib)
        copy = pltpu.make_async_copy(amps.at[:, mine], home, local0.at[s])
        copy.start()
        here[s] = copy
    send(tiles, tiles_sib.at[pl.ds(0, SLOTS)], misc.at[2], misc.at[3], sib)
    own_tiles = pltpu.make_async_copy(tiles, tiles_own.at[pl.ds(0, SLOTS)], misc.at[4])
    own_tiles.start()
    for ref in (tiles_own, tiles_sib):
        ref[SLOTS] = jnp.zeros((TILE, TILE), ref.dtype)
    history[0] = jnp.zeros((TILE, WIDE), jnp.float32)

    def region(s, phase, index, half):
        axis = ORDERS[s][phase]
        done = ORDERS[s][:phase]
        pick = [slice(None) if a in done else at[a] for a in (Y, Z, X)]
        pick[axis] = index
        return gathered[s].at[pick[Y], half, pick[Z], pick[X]]

    def spread(s, phase):
        axis = ORDERS[s][phase]
        mine = region(s, phase, at[axis], slice(None))
        for n, by in enumerate(steps):
            send(mine, mine, send_ag.at[s, phase * 3 + n], recv_ag.at[s, phase * 3 + n], peer(axis, by))

    def finish(s, phase):
        axis = ORDERS[s][phase]
        for n, by in enumerate(steps):
            ref = region(s, phase, turn(at[axis], -by), slice(None))
            arrive(ref, send_ag.at[s, phase * 3 + n], recv_ag.at[s, phase * 3 + n], peer(axis, by))

    def last_spread(s):
        axis = ORDERS[s][2]
        for turn_of in range(2):
            for way, by in enumerate((1, -1)):
                n = 6 + way * 2 + turn_of
                mine = region(s, 2, at[axis], way ^ turn_of)
                send(mine, mine, send_ag.at[s, n], recv_ag.at[s, n], peer(axis, by))

    def last_forward(s):
        axis = ORDERS[s][2]
        for way, by in enumerate((1, -1)):
            n = 6 + way * 2
            passed = region(s, 2, turn(at[axis], -by), way)
            arrive(passed, send_ag.at[s, n], recv_ag.at[s, n], peer(axis, by))
            send(passed, passed, send_ag.at[s, 10 + way], recv_ag.at[s, 10 + way], peer(axis, by))

    def last_rest(s):
        axis = ORDERS[s][2]
        for way, by in enumerate((1, -1)):
            n = 7 + way * 2
            arrive(region(s, 2, turn(at[axis], -by), 1 - way), send_ag.at[s, n], recv_ag.at[s, n], peer(axis, by))

    def last_finish(s):
        axis = ORDERS[s][2]
        for way, by in enumerate((1, -1)):
            arrive(region(s, 2, turn(at[axis], 2), way), send_ag.at[s, 10 + way], recv_ag.at[s, 10 + way], peer(axis, by))

    def first(s):
        here[s].wait()
        arrive(gathered[s].at[y, 1 - core, z, x], send0.at[s], recv0.at[s], sib)
        spread(s, 0)

    def second(s):
        finish(s, 0)
        spread(s, 1)

    def third(s):
        finish(s, 1)
        last_spread(s)

    def slots_sent(_):
        for n, row_of in enumerate(slot_lists(named[...])):
            lists_out[n : n + 1, :] = row_of
        for n in range(10, 16):
            lists_out[n : n + 1, :] = jnp.zeros((1, SLOTS), jnp.int32)
        send(lists_out, lists_in, misc.at[0], misc.at[1], sib)
        to_scalar = pltpu.make_async_copy(lists_out, lists, misc.at[6])
        to_scalar.start()
        to_scalar.wait()

    def slots_ready(_):
        own_tiles.wait()
        arrive(tiles_sib.at[pl.ds(0, SLOTS)], misc.at[2], misc.at[3], sib)
        arrive(lists_in, misc.at[0], misc.at[1], sib)
        to_scalar = pltpu.make_async_copy(lists_in, lists_sib, misc.at[5])
        to_scalar.start()
        to_scalar.wait()

    def products(k, group):
        which, tile_ref = ((lists, tiles_own), (lists_sib, tiles_sib))[group]
        subs = CHUNK_SUBS[k]
        wide = len(subs) * LANES

        def step(q, carry):
            left, right = [], []
            for g in range(GROUP):
                left.append(tile_ref[which[g, q]])
                m = which[GROUP + g, q]
                right.append(jnp.concatenate([slices[s][m] for s in subs], axis=1))
            new = jnp.dot(
                jnp.concatenate(left, axis=1), jnp.concatenate(right, axis=0), preferred_element_type=jnp.float32
            )
            history[q + 1, :, :wide] = history[which[8, q], :, :wide] + new
            return carry

        lax.fori_loop(0, QUADS, step, 0, unroll=12)
        for o in range(OUTS):
            total = history[which[9, o], :, :wide]
            for n, s in enumerate(subs):
                rows_ref = part.at[s, group].reshape(OUTS * TILE, LANES)
                rows_ref[o * TILE : (o + 1) * TILE, :] = total[:, n * LANES : (n + 1) * LANES]

    def mine_of(k, g, b, axis, index):
        return [
            part[s, g, b, index, i] if axis == Z else part[s, g, b, i, index] for i in range(RING) for s in CHUNK_SUBS[k]
        ]

    def sum_send(k, g):
        axis = SUM_ORDERS[g][0]
        rows = message(RING * len(CHUNK_SUBS[k]))
        for way, by in enumerate((1, -1)):
            encode(far_out.at[k, g, way], mine_of(k, g, way, axis, turn(at[axis], 2)))
            send(far_out.at[k, g, way, rows], far_in.at[k, g, way, rows], send1.at[k, g, way], recv1.at[k, g, way], peer(axis, by))
        for way, by in enumerate((1, -1)):
            n = 2 + way
            encode(near_out.at[k, g, way], mine_of(k, g, 1 - way, axis, turn(at[axis], by)))
            send(near_out.at[k, g, way, rows], got1.at[k, g, way, 1 - way, rows], send1.at[k, g, n], recv1.at[k, g, n], peer(axis, by))

    def sum_relay(k, g):
        axis = SUM_ORDERS[g][0]
        blocks = RING * len(CHUNK_SUBS[k])
        rows = message(blocks)
        for way, by in enumerate((1, -1)):
            n = 4 + way
            arrive(far_in.at[k, g, way, rows], send1.at[k, g, way], recv1.at[k, g, way], peer(axis, by))
            own = mine_of(k, g, way, axis, turn(at[axis], by))
            encode(mid_out.at[k, g, way], [a + b for a, b in zip(own, decode(far_in.at[k, g, way], blocks))])
            send(mid_out.at[k, g, way, rows], got1.at[k, g, way, way, rows], send1.at[k, g, n], recv1.at[k, g, n], peer(axis, by))

    def sum_pass(k, g):
        axis, then = SUM_ORDERS[g]
        subs = CHUNK_SUBS[k]
        blocks = RING * len(subs)
        rows = message(blocks)
        for way, by in enumerate((1, -1)):
            for n, b in ((2, 1 - way), (4, way)):
                arrive(got1.at[k, g, way, b, rows], send1.at[k, g, n + way], recv1.at[k, g, n + way], peer(axis, by))
        for b in range(NB):
            own = mine_of(k, g, b, axis, at[axis])
            one, two = (decode(got1.at[k, g, way, b], blocks) for way in range(2))
            for j in range(blocks):
                sum1[subs[j % len(subs)], g, b, j // len(subs)] = own[j] + (one[j] + two[j])
        rows = message(NB * len(subs))
        for n, by in enumerate(steps):
            index = turn(at[then], by)
            encode(next_out.at[k, g, n], [sum1[s, g, b, index] for b in range(NB) for s in subs])
            send(next_out.at[k, g, n, rows], got2.at[k, g, n, rows], send2.at[k, g, n], recv2.at[k, g, n], peer(then, by))

    def sum_end(k, g):
        then = SUM_ORDERS[g][1]
        subs = CHUNK_SUBS[k]
        blocks = NB * len(subs)
        rows = message(blocks)
        for n, by in enumerate(steps):
            arrive(got2.at[k, g, n, rows], send2.at[k, g, n], recv2.at[k, g, n], peer(then, by))
        got = [decode(got2.at[k, g, n], blocks) for n in range(3)]
        own = [sum1[s, g, b, at[then]] for b in range(NB) for s in subs]
        deliver(g, subs, [(own[j] + got[0][j]) + (got[1][j] + got[2][j]) for j in range(blocks)])

    def all_send(k, g):
        rows = message(NB * len(CHUNK_SUBS[k]))
        for n, (dz, dx) in enumerate(AWAY):
            to_z, to_x = turn(z, dz), turn(x, dx)
            encode(all_out.at[g, n], [part[s, g, b, to_z, to_x] for b in range(NB) for s in CHUNK_SUBS[k]])
            to = (row, to_z * RING + to_x)
            send(all_out.at[g, n, rows], all_in.at[g, n, rows], send_all.at[g, n], recv_all.at[g, n], to)

    def all_end(k, g):
        subs = CHUNK_SUBS[k]
        blocks = NB * len(subs)
        rows = message(blocks)
        totals = [part[s, g, b, z, x] for b in range(NB) for s in subs]
        for n, (dz, dx) in enumerate(AWAY):
            to = (row, turn(z, dz) * RING + turn(x, dx))
            arrive(all_in.at[g, n, rows], send_all.at[g, n], recv_all.at[g, n], to)
            totals = [a + b for a, b in zip(totals, decode(all_in.at[g, n], blocks))]
        deliver(g, subs, totals)

    def deliver(g, subs, totals):
        for j, total in enumerate(totals):
            b, s = j // len(subs), subs[j % len(subs)]
            if g == 1:
                cross_out[s, b] = total
            else:
                columns = pl.ds(pl.multiple_of(core * (SUBS * LANES) + s * LANES, LANES), LANES)
                owned[b, :, columns] = divided(total, b, columns)
        if g == 1:
            for s in subs:
                send(cross_out.at[s], cross_in.at[s], send_x.at[s], recv_x.at[s], sib)

    def sum_cross(s):
        arrive(cross_in.at[s], send_x.at[s], recv_x.at[s], sib)
        for b in range(NB):
            columns = pl.ds(pl.multiple_of((1 - core) * (SUBS * LANES) + s * LANES, LANES), LANES)
            owned[b, :, columns] = divided(cross_in[s, b], b, columns)

    def unit(work):
        return lambda n: work(n // 2, n % 2)

    fwd, rest, done = last_forward, last_rest, last_finish
    mul, out, mid, add, end = (unit(w) for w in (products, sum_send, sum_relay, sum_pass, sum_end))
    far_send, far_end = unit(all_send), unit(all_end)
    plan = [(first, s) for s in (0, 1, 3, 2)] + [(slots_sent, 0)] + [(second, s) for s in (0, 1, 3, 2)]
    plan += [(first, s) for s in (4, 5, 6, 7)] + [(third, s) for s in (0, 1, 3)]
    plan += [(second, s) for s in (6, 7, 4, 5)] + [(slots_ready, 0)]
    plan += [(fwd, 0), (fwd, 1), (fwd, 3), (rest, 0), (third, 2), (rest, 1), (third, 4), (rest, 3), (third, 5)]
    plan += [(done, 0), (done, 1), (mul, 0), (out, 0)]
    plan += [(fwd, 2), (mul, 1), (out, 1), (mid, 0)]
    plan += [(rest, 2), (third, 6), (fwd, 4), (fwd, 5), (done, 2), (done, 3), (mul, 2), (out, 2), (mid, 1), (add, 0)]
    plan += [(third, 7), (mul, 3), (out, 3), (mid, 2), (add, 1), (fwd, 6)]
    plan += [(rest, 4), (rest, 5), (done, 4), (done, 5), (mul, 4), (out, 4), (mid, 3), (add, 2), (end, 0), (fwd, 7)]
    plan += [(mul, 5), (out, 5), (mid, 4), (add, 3), (end, 1)]
    plan += [(rest, 6), (rest, 7), (done, 6), (done, 7), (mul, 6), (out, 6), (mid, 5), (add, 4), (end, 2)]
    plan += [(mul, 7), (out, 7), (mid, 6), (add, 5), (end, 3), (mid, 7), (add, 6), (end, 4), (end, 5), (add, 7), (end, 6), (end, 7)]
    for work, which in plan:
        work(which)
    for s in range(SUBS):
        sum_cross(s)
    for copy in sent:
        copy.wait_send()


def owned_update(named, virt, b_level, pair, amplitudes, tiles):
    dma = pltpu.SemaphoreType.DMA
    vmem = pltpu.VMEM
    f32 = jnp.float32
    scratch = [vmem((2 * NT, TILE, LANES), jnp.bfloat16) for _ in range(SUBS)]
    scratch += [
        vmem((SLOTS + 1, TILE, TILE), jnp.bfloat16),
        vmem((SLOTS + 1, TILE, TILE), jnp.bfloat16),
        vmem((QUADS + 1, TILE, WIDE), f32),
        vmem((SUBS, 2, NB, RING, RING, OWN, LANES), f32),
        vmem((CHUNKS, 2, 2, RING * OWN + 8, LANES), jnp.int32),
        vmem((CHUNKS, 2, 2, RING * OWN + 8, LANES), jnp.int32),
        vmem((CHUNKS, 2, 2, RING * OWN + 8, LANES), jnp.int32),
        vmem((CHUNKS, 2, 2, RING * OWN + 8, LANES), jnp.int32),
        vmem((CHUNKS, 2, 2, NB, RING * OWN + 8, LANES), jnp.int32),
        vmem((SUBS, 2, NB, RING, OWN, LANES), f32),
        vmem((CHUNKS, 2, 3, NB * OWN + 8, LANES), jnp.int32),
        vmem((CHUNKS, 2, 3, NB * OWN + 8, LANES), jnp.int32),
        vmem((2, 15, NB // 2 * OWN + 8, LANES), jnp.int32),
        vmem((2, 15, NB // 2 * OWN + 8, LANES), jnp.int32),
        vmem((SUBS, NB, OWN, LANES), f32),
        vmem((SUBS, NB, OWN, LANES), f32),
        vmem((16, 128), jnp.int32),
        vmem((16, 128), jnp.int32),
        pltpu.SMEM((16, 128), jnp.int32),
        pltpu.SMEM((16, 128), jnp.int32),
        dma((SUBS,)), dma((SUBS,)), dma((SUBS,)),
        dma((SUBS, 16)), dma((SUBS, 16)),
        dma((CHUNKS, 2, 6)), dma((CHUNKS, 2, 6)), dma((CHUNKS, 2, 3)), dma((CHUNKS, 2, 3)),
        dma((SUBS,)), dma((SUBS,)), dma((2, 15)), dma((2, 15)), dma((8,)),
    ]
    return pl.pallas_call(
        ladder_kernel,
        out_shape=jax.ShapeDtypeStruct((NB, OWN, 2 * SUBS * LANES), f32),
        in_specs=[
            pl.BlockSpec(memory_space=pltpu.VMEM),
            pl.BlockSpec(memory_space=pltpu.VMEM),
            pl.BlockSpec(memory_space=pltpu.SMEM),
            pl.BlockSpec(memory_space=pltpu.VMEM),
            pl.BlockSpec(memory_space=pl.ANY),
            pl.BlockSpec(memory_space=pl.ANY),
        ],
        out_specs=pl.BlockSpec(memory_space=pltpu.VMEM),
        scratch_shapes=scratch,
        compiler_params=pltpu.CompilerParams(
            collective_id=0, has_side_effects=True, vmem_limit_bytes=60 * 1024 * 1024
        ),
        name="ladder",
    )(named, virt, b_level, pair, amplitudes, tiles)


def per_device(amplitudes, integrals, slot_index, virt_energy, b_energy, pair_energy):
    named = slot_index[0].transpose(1, 2, 0)
    tiles = integrals.reshape(-1, TILE, TILE)
    return owned_update(named, virt_energy[None, :], b_energy, pair_energy[None, :], amplitudes, tiles)


def solution(mesh):
    placed = (
        P(("row", "col"), None),
        P(("row", "col"), None, None, None, None),
        P(("row", "col"), None, None, None),
        P(("row", "col")),
        P(),
        P(),
    )
    return jax.shard_map(
        per_device,
        mesh=mesh,
        in_specs=placed,
        out_specs=P(None, ("row", "col"), None),
        check_vma=False,
    )
```
